256 devices in a mesh: seq: 64 (over z, x, core), rep: 4 (over y).
Axes of the slice: x: 4, y: 4, z: 8, core: 2. Of those that a mesh axis runs over, the one named last changes fastest.
Arguments:
- frames: bfloat16 [65536, 1536], P(('rep', 'seq')), parts along dimension 0, may hold values from -6 to 6
- lengths: int32 [512], P('rep'), parts along dimension 0, may hold values from 1 to 256, 16384 in all
- norm_attn: float32 [1536], replicated, may hold values from 0.25 to 1.75
- w_query: bfloat16 [1536, 768], P('seq'), may hold values from -2 to 2, as said below
- w_key: bfloat16 [1536, 768], P('seq'), may hold values from -2 to 2, as said below
- w_value: bfloat16 [1536, 768], P('seq'), may hold values from -0.15625 to 0.15625
- w_out: bfloat16 [768, 1536], P('seq'), may hold values from -0.21875 to 0.21875
- norm_conv: float32 [1536], replicated, may hold values from 0.25 to 1.75
- w_expand: bfloat16 [1536, 1536], P('seq'), may hold values from -0.15625 to 0.15625
- kernel: float32 [31, 768], replicated, may hold values from -1 to 1
- bn_gain: float32 [768], replicated, may hold values from 0.25 to 1.75
- bn_bias: float32 [768], replicated, may hold values from -3 to 3
- w_shrink: bfloat16 [768, 1536], P('seq'), may hold values from -0.21875 to 0.21875
- norm_final: float32 [1536], replicated, may hold values from 0.25 to 1.75
Outputs:
- block_out: bfloat16 [65536, 1536], P(('rep', 'seq')), parts along dimension 0
- pooled: float32 [512, 1536], P('rep'), parts along dimension 0
The draws below stay inside these ranges and needn't reach their ends.
There are 4 independent parts, one for each index of `rep`. The reference program is written for one: setup_inputs(seed, part) draws one part's arguments, and reference() takes and returns one part's arrays. A program takes and returns all parts, laid end to end along the dimension named above; an argument that names none is the same for every part. Nothing has to cross between parts.
Inputs may be any that keep to these rules, and one draw needn't show every extreme that they name: The lengths of the recordings sum to 16384. `w_query`: entries of order 1536**-0.5. `w_key`: entries of order 1536**-0.5.
All inputs are finite; a program needn't handle non-finite values.
Results may differ from the reference program's by a relative error of at most 0.013.
Values may be sent and summed in bfloat16 or wider, within the bound.
A program may use at most 64 MiB of HBM per device.

```python
import math
import jax
import jax.numpy as jnp
import numpy as np
from jax import lax

D = 1536
H = 8
HD = 96
CH = 768
KERNEL = 31
TOK_DEV = 256
HH = 768
TOKENS = 16384
NREC = 128
N_SEQ = 64


def draw_w_query(key, part):
    key = jax.random.fold_in(key, 11)
    own = jax.random.normal(key, (D, H * HD), jnp.float32)
    return jnp.clip(own * D ** (-0.5), -2.0, 2.0).astype(jnp.bfloat16)


def draw_w_key(key, part):
    key = jax.random.fold_in(key, 23)
    own = jax.random.normal(key, (D, H * HD), jnp.float32)
    return jnp.clip(own * D ** (-0.5), -2.0, 2.0).astype(jnp.bfloat16)


def steps_of(own_key, dims, split, smallest, top_value):
    loudness = 1.0
    for axis_at, shards_of in split:
        heights = jax.random.uniform(jax.random.fold_in(jax.random.fold_in(own_key, 6), axis_at), (shards_of,), jnp.float32, smallest / len(split), top_value / len(split))
        loudness = loudness * jnp.repeat(jnp.exp(heights), dims[axis_at] // shards_of).reshape((-1,) + (1,) * (len(dims) - 1 - axis_at))
    return loudness


def length_profile(number_of, total, limit, skew):
    loads = [(1 << 20) // math.isqrt(rank ** skew) + 1 for rank in range(2, number_of + 1)]
    surplus, holding = total - limit - (number_of - 1), [1] * (number_of - 1)
    while surplus > 0:
        candidates = [i for i in range(number_of - 1) if holding[i] < limit]
        pool, left = sum([loads[i] for i in candidates]), surplus
        for i in candidates:
            addition = min(limit - holding[i], max(1, left * loads[i] // pool), surplus)
            holding[i] = holding[i] + addition
            surplus = surplus - addition
    return np.array([limit] + holding)


def uneven(rng, count, total, limit, lean):
    if count == 2:
        one = jax.random.randint(rng, (), max(1, total - limit), min(limit, total - 1) + 1)
        return jnp.stack([one, total - one])
    sizes = jnp.asarray(length_profile(count, total, limit, lean), jnp.int32)
    couples = (count - 1) // 2
    donor, taker = sizes[1:1 + 2 * couples:2], sizes[2:2 + 2 * couples:2]
    room = jnp.minimum(donor - 1, limit - taker)
    passed = jax.random.randint(jax.random.fold_in(rng, 1), (couples,), 0, 1 << 20) % (room + 1)
    sizes = sizes.at[1:1 + 2 * couples:2].set(donor - passed).at[2:2 + 2 * couples:2].set(taker + passed)
    return sizes[jax.random.permutation(jax.random.fold_in(rng, 2), count)]


def gaussian(stream_key, shape, deviation, most, pieces=(), kind=jnp.bfloat16):
    drawn = jax.random.normal(stream_key, shape, jnp.float32) * deviation
    if len(pieces) > 0:
        drawn = steps_of(stream_key, shape, pieces, -0.22, 0.18) * drawn
    return jnp.clip(drawn, min=-most, max=most).astype(kind)


def setup_inputs(seed: int = 0, part: int = 0) -> dict:
    key_list = jax.random.split(jax.random.key(seed), 15)
    own_keys = jax.random.split(jax.random.fold_in(key_list[14], part), 15)
    return {
        "frames": gaussian(own_keys[0], (TOKENS, D), 1.0, 6.0, ((0, 64),)),
        "lengths": uneven(own_keys[1], NREC, TOKENS, TOK_DEV, 2).astype(jnp.int32),
        "norm_attn": jnp.clip(1.0 + 0.15 * jax.random.normal(key_list[2], (D,), jnp.float32), 0.25, 1.75),
        "w_query": draw_w_query(jax.random.fold_in(key_list[14], 71), part),
        "w_key": draw_w_key(jax.random.fold_in(key_list[14], 71), part),
        "w_value": gaussian(key_list[5], (D, HH), D ** -0.5, 0.15625, ((0, 64),)),
        "w_out": gaussian(key_list[6], (HH, D), HH ** -0.5, 0.21875, ((0, 64),)),
        "norm_conv": jnp.clip(1.0 + 0.15 * jax.random.normal(key_list[7], (D,), jnp.float32), 0.25, 1.75),
        "w_expand": gaussian(key_list[8], (D, 2 * CH), D ** -0.5, 0.15625, ((0, 64),)),
        "kernel": gaussian(key_list[9], (KERNEL, CH), KERNEL ** -0.5, 1.0, (), jnp.float32),
        "bn_gain": jnp.clip(1.0 + 0.15 * jax.random.normal(key_list[10], (CH,), jnp.float32), 0.25, 1.75),
        "bn_bias": gaussian(key_list[11], (CH,), 0.5, 3.0, (), jnp.float32),
        "w_shrink": gaussian(key_list[12], (CH, D), CH ** -0.5, 0.21875, ((0, 64),)),
        "norm_final": jnp.clip(1.0 + 0.15 * jax.random.normal(key_list[13], (D,), jnp.float32), 0.25, 1.75),
    }


def layer_norm(values, gain):
    mean = lax.optimization_barrier(jnp.mean(values, axis=-1, keepdims=True))
    centred = values - mean
    var = lax.optimization_barrier(jnp.mean(centred * centred, axis=-1, keepdims=True))
    return centred * lax.rsqrt(var + 1e-05) * gain

def segment_of(lengths, count):
    ends = jnp.cumsum(lengths).astype(jnp.int32)
    places = jnp.arange(count, dtype=jnp.int32)
    return lax.optimization_barrier(jnp.sum((ends[None, :] <= places[:, None]).astype(jnp.int32), axis=1)).astype(jnp.int32)

def reference(frames, lengths, norm_attn, w_query, w_key, w_value, w_out, norm_conv, w_expand, kernel, bn_gain, bn_bias, w_shrink, norm_final):
    segment = segment_of(lengths, TOKENS)
    normed = layer_norm(frames.astype(jnp.float32), norm_attn).astype(jnp.bfloat16)
    query = jnp.dot(normed, w_query, preferred_element_type=jnp.float32).astype(jnp.bfloat16)
    key = jnp.dot(normed, w_key, preferred_element_type=jnp.float32).astype(jnp.bfloat16)
    value = jnp.dot(normed, w_value, preferred_element_type=jnp.float32).astype(jnp.bfloat16)
    pad_rows = jnp.zeros((TOK_DEV, HH), key.dtype)
    key_pad = jnp.concatenate([pad_rows, key, pad_rows], axis=0)
    value_pad = jnp.concatenate([pad_rows, value, pad_rows], axis=0)
    minus = -jnp.ones((TOK_DEV,), jnp.int32)
    seg_pad = jnp.concatenate([minus, segment, minus], axis=0).astype(jnp.int32)
    scale = 1.0 / HD ** 0.5

    def one_block(block):
        start = (block * TOK_DEV).astype(jnp.int32)
        q_blk = lax.dynamic_slice_in_dim(query, start, TOK_DEV, 0).reshape(TOK_DEV, H, HD).astype(jnp.float32)
        k_blk = lax.dynamic_slice_in_dim(key_pad, start, 3 * TOK_DEV, 0).reshape(3 * TOK_DEV, H, HD).astype(jnp.float32)
        v_blk = lax.dynamic_slice_in_dim(value_pad, start, 3 * TOK_DEV, 0).reshape(3 * TOK_DEV, H, HD).astype(jnp.float32)
        seg_q = lax.dynamic_slice_in_dim(segment, start, TOK_DEV, 0)
        seg_k = lax.dynamic_slice_in_dim(seg_pad, start, 3 * TOK_DEV, 0)
        score = jnp.einsum('qhd,khd->hqk', q_blk, k_blk) * scale
        score = jnp.where((seg_q[:, None] == seg_k[None, :])[None], score, -1e+30)
        top = lax.optimization_barrier(jnp.max(score, axis=-1, keepdims=True))
        expo = jnp.exp(score - top)
        weights = (expo / lax.optimization_barrier(jnp.sum(expo, axis=-1, keepdims=True))).astype(jnp.bfloat16)
        ctx = jnp.einsum('hqk,khd->qhd', weights.astype(jnp.float32), v_blk)
        return ctx.astype(jnp.bfloat16).reshape(TOK_DEV, HH)
    context = lax.map(one_block, jnp.arange(N_SEQ, dtype=jnp.int32)).reshape(TOKENS, HH)
    attn = jnp.dot(context, w_out, preferred_element_type=jnp.float32)
    after_attn = (frames.astype(jnp.float32) + attn).astype(jnp.bfloat16)
    conv_in = layer_norm(after_attn.astype(jnp.float32), norm_conv).astype(jnp.bfloat16)
    expanded = jnp.dot(conv_in, w_expand, preferred_element_type=jnp.float32)
    glu = (expanded[:, :CH] * jax.nn.sigmoid(expanded[:, CH:])).astype(jnp.bfloat16)
    half = (KERNEL - 1) // 2
    glu_pad = jnp.concatenate([jnp.zeros((half, CH), glu.dtype), glu, jnp.zeros((half, CH), glu.dtype)], axis=0)
    rim = -jnp.ones((half,), jnp.int32)
    seg_rim = jnp.concatenate([rim, segment, rim], axis=0).astype(jnp.int32)
    depth = jnp.zeros((TOKENS, CH), jnp.float32)
    for tap in range(KERNEL):
        source = glu_pad[tap:tap + TOKENS].astype(jnp.float32)
        same = (seg_rim[tap:tap + TOKENS] == segment)[:, None]
        depth = depth + kernel[tap][None, :] * jnp.where(same, source, 0.0)
    moved = depth * bn_gain + bn_bias
    activated = (moved * jax.nn.sigmoid(moved)).astype(jnp.bfloat16)
    shrunk = jnp.dot(activated, w_shrink, preferred_element_type=jnp.float32)
    block_out = layer_norm(after_attn.astype(jnp.float32) + shrunk, norm_final).astype(jnp.bfloat16)
    sums = jax.ops.segment_sum(block_out.astype(jnp.float32), segment, NREC)
    pooled = sums / lengths.astype(jnp.float32)[:, None]
    return (block_out, pooled)
```

```python
import functools

import jax
import jax.numpy as jnp
from jax import lax
from jax.experimental import pallas as pl
from jax.experimental.pallas import tpu as pltpu
from jax.sharding import PartitionSpec as P

H = 8
HD = 96
KERNEL = 31
MESH = pl.DeviceIdType.MESH
NZ, NX = 8, 4
UNIT = 1152
COLS = 7 * UNIT
GROUPS = ((0, 3 * UNIT), (3 * UNIT, 4 * UNIT), (4 * UNIT, 6 * UNIT), (6 * UNIT, 7 * UNIT))
X_FIRST = (1408, 512, 896, 512)
N_COPIES = 320


class Place:
    def __init__(self):
        index = lax.axis_index("seq")
        self.z = index // 8
        self.x = (index // 2) % 4
        self.c = index % 2

    def at(self, dz, dx, dc=0):
        z = (self.z + dz + NZ) % NZ
        x = (self.x + dx + NX) % NX
        c = (self.c + dc) % 2
        return {"seq": z * 8 + x * 2 + c}


class Copies:
    def __init__(self, ref, send_sem, recv_sem):
        self.ref, self.send_sem, self.recv_sem = ref, send_sem, recv_sem
        self.all = []

    def send(self, region, device):
        k = len(self.all)
        part = self.ref.at[region]
        copy = pltpu.make_async_remote_copy(
            src_ref=part,
            dst_ref=part,
            send_sem=self.send_sem.at[k],
            recv_sem=self.recv_sem.at[k],
            device_id=device,
            device_id_type=MESH,
        )
        copy.start()
        self.all.append(copy)
        return copy

    def finish(self):
        for copy in self.all:
            copy.wait_send()


def ring(copies, place, axis, region, shared):
    n = NZ if axis == "z" else NX
    me = place.z if axis == "z" else place.x
    up = place.at(1, 0) if axis == "z" else place.at(0, 1)
    down = place.at(-1, 0) if axis == "z" else place.at(0, -1)
    other = place.at(0, 0, 1)
    forth = copies.send(region(me, None), up)
    back = copies.send(region(me, None), down)
    for step in range(1, n // 2):
        low, high = (me - step + n) % n, (me + step) % n
        last = step == n // 2 - 1
        yield
        forth.wait_recv()
        forth = copies.send(region(low, 0 if last else None), up)
        shared.append(copies.send(region(low, None), other))
        back.wait_recv()
        back = copies.send(region(high, 1 if last else None), down)
        shared.append(copies.send(region(high, None), other))
    yield
    forth.wait_recv()
    back.wait_recv()
    shared.append(copies.send(region((me + n // 2) % n, None), other))


def gather(copies, place, group, split, shared):
    lo, hi = group
    mid = lo + split

    def cut(a, b, half):
        if half is None:
            return pl.ds(a, b - a)
        m = (a + b) // 256 * 128
        return pl.ds(a, m - a) if half == 0 else pl.ds(m, b - m)

    def part(a, b, first):
        def one(k, half):
            at = (place.z, k) if first == "x" else (k, place.x)
            return (at[0], at[1], place.c, slice(None), cut(a, b, half))

        def line(k, half):
            at = (k, slice(None)) if first == "x" else (slice(None), k)
            return (at[0], at[1], place.c, slice(None), cut(a, b, half))

        yield from ring(copies, place, first, one, shared)
        yield from ring(copies, place, "z" if first == "x" else "x", line, shared)

    return part(lo, mid, "x"), part(mid, hi, "z")


def fold(rows8):
    half = rows8.shape[1] // 2
    return jnp.concatenate([rows8[:, :half], rows8[:, half:]], axis=0)


def pack_own(g_ref, place, units, first):
    for unit, value in units:
        main = jnp.where(first, value[:16], value[8:])
        rest = jnp.where(first, value[16:], value[:8])
        whole = jnp.concatenate([main, fold(rest)], axis=1).astype(jnp.bfloat16)
        g_ref[place.z, place.x, place.c, :, unit * UNIT : (unit + 1) * UNIT] = whole


def gather_kernel(wq, wk, wv, wo, we, ws, out_ref, g_ref, give, take, send_sem, recv_sem, side_sem, out_sem):
    place = Place()
    f32 = jnp.float32
    barrier = pltpu.get_barrier_semaphore()
    partners = [place.at(1, 0), place.at(-1, 0), place.at(0, 1), place.at(0, -1), place.at(0, 0, 1)]
    for partner in partners:
        pl.semaphore_signal(barrier, inc=1, device_id=partner, device_id_type=MESH)
    for k, ref in enumerate((wo, ws)):
        value = ref[...].astype(f32)
        mine = jnp.where(place.c == 0, value[:, 768:], value[:, :768])
        give[k] = jnp.concatenate([mine, jnp.zeros((4, 768), f32)], axis=0).astype(jnp.bfloat16)
    units = [(0, wq[...]), (1, wk[...]), (2, wv[...]), (4, we[:, :768]), (5, we[:, 768:])]
    pack_own(g_ref, place, [(u, v.astype(f32)) for u, v in units], place.c == 0)
    pl.semaphore_wait(barrier, len(partners))
    side = pltpu.make_async_remote_copy(
        src_ref=give, dst_ref=take, send_sem=side_sem.at[0], recv_sem=side_sem.at[1],
        device_id=place.at(0, 0, 1), device_id_type=MESH,
    )
    side.start()
    copies = Copies(g_ref, send_sem, recv_sem)
    shared = []
    other = place.at(0, 0, 1)

    def start(group):
        lo, hi = GROUPS[group]
        shared.append(copies.send((place.z, place.x, place.c, slice(None), pl.ds(lo, hi - lo)), other))
        return list(gather(copies, place, GROUPS[group], X_FIRST[group], shared))

    live = start(0)
    live += start(2)
    for g in live:
        next(g, None)
    side.wait()
    units = []
    for k, (unit, ref) in enumerate(((3, wo), (6, ws))):
        value = ref[...].astype(f32)
        own = jnp.where(place.c == 0, value[:, :768], value[:, 768:])
        got = take[k].astype(f32)[:12]
        units.append((unit, jnp.where(place.c == 0, jnp.concatenate([own, got], axis=0), jnp.concatenate([got, own], axis=0))))
    pack_own(g_ref, place, units, place.x % 2 == 0)
    more = start(1) + start(3)
    for g in more:
        next(g, None)
    live += more
    while live:
        live = [g for g in live if next(g, True) is None]
    for copy in shared:
        copy.wait_recv()
    out = pltpu.make_async_copy(g_ref, out_ref, out_sem)
    out.start()
    copies.finish()
    out.wait()


def gather_weights(wq, wk, wv, wo, we, ws):
    return pl.pallas_call(
        gather_kernel,
        out_shape=jax.ShapeDtypeStruct((NZ, NX, 2, 16, COLS), jnp.bfloat16),
        in_specs=[pl.BlockSpec(memory_space=pltpu.VMEM)] * 6,
        out_specs=pl.BlockSpec(memory_space=pl.ANY),
        scratch_shapes=[
            pltpu.VMEM((NZ, NX, 2, 16, COLS), jnp.bfloat16),
            pltpu.VMEM((2, 16, 768), jnp.bfloat16),
            pltpu.VMEM((2, 16, 768), jnp.bfloat16),
            pltpu.SemaphoreType.DMA((N_COPIES,)),
            pltpu.SemaphoreType.DMA((N_COPIES,)),
            pltpu.SemaphoreType.DMA((2,)),
            pltpu.SemaphoreType.DMA,
        ],
        compiler_params=pltpu.CompilerParams(
            collective_id=0, has_side_effects=True, vmem_limit_bytes=48 << 20
        ),
    )(wq, wk, wv, wo, we, ws)


def unpack(g, unit, out_rows):
    piece = g[..., unit * UNIT : (unit + 1) * UNIT]
    main = piece[..., :768]
    rest = piece[..., 768:].reshape(NZ, NX, 2, 2, 8, 384).transpose(0, 1, 2, 4, 3, 5).reshape(NZ, NX, 2, 8, 768)
    ahead = jnp.concatenate([main, rest], axis=3)
    behind = jnp.concatenate([rest, main], axis=3)
    if not out_rows:
        both = jnp.stack([ahead[:, :, 0], behind[:, :, 1]], axis=2)
        return both.reshape(1536, 768)
    both = jnp.stack([ahead[:, 0::2], behind[:, 1::2]], axis=2)
    return both.transpose(0, 1, 2, 4, 3, 5).reshape(768, 1536)


def extended(block, sides, width):
    for axis, dim in sides:
        count = lax.axis_size(axis)
        forward = [(i, i + 1) for i in range(count - 1)]
        backward = [(target, source) for source, target in forward]
        low = lax.ppermute(
            lax.slice_in_dim(block, block.shape[dim] - width, None, axis=dim), axis, forward
        )
        high = lax.ppermute(lax.slice_in_dim(block, 0, width, axis=dim), axis, backward)
        block = jnp.concatenate([low, block, high], axis=dim)
    return block


def layer_norm(values, gain):
    mean = jnp.mean(values, axis=-1, keepdims=True)
    centred = values - mean
    var = jnp.mean(centred * centred, axis=-1, keepdims=True)
    return centred * lax.rsqrt(var + 1e-05) * gain


def segment_at(ends, places):
    found = jnp.sum((ends[None, :] <= places[:, None]).astype(jnp.int32), axis=1)
    inside = (places >= 0) & (places < ends[-1])
    return jnp.where(inside, found, -1)


def add_rows(left, piece):
    return jnp.dot(left, piece, preferred_element_type=jnp.float32)


def depthwise(glu_rim, seg_rim, seg_mid, taps, count):
    depth = jnp.zeros((count, glu_rim.shape[1]), jnp.float32)
    for tap in range(KERNEL):
        source = glu_rim[tap : tap + count].astype(jnp.float32)
        same = (seg_rim[tap : tap + count] == seg_mid)[:, None]
        depth = depth + taps[tap][None, :] * jnp.where(same, source, 0.0)
    return depth


def local(
    frames,
    lengths,
    norm_attn,
    w_query,
    w_key,
    w_value,
    w_out,
    norm_conv,
    w_expand,
    kernel,
    bn_gain,
    bn_bias,
    w_shrink,
    norm_final,
):
    index = lax.axis_index("seq")
    rows = frames.shape[0]
    half = (KERNEL - 1) // 2
    ends = jnp.cumsum(lengths)
    first = index * rows
    seg_own = segment_at(ends, first + jnp.arange(rows, dtype=jnp.int32))
    normed = layer_norm(frames.astype(jnp.float32), norm_attn).astype(jnp.bfloat16)

    def add_one(piece):
        return add_rows(normed, piece)

    g = gather_weights(w_query, w_key, w_value, w_out, w_expand, w_shrink)
    query = add_one(unpack(g, 0, False))
    key = add_one(unpack(g, 1, False))
    value = add_one(unpack(g, 2, False))
    query = query.astype(jnp.bfloat16)
    stacked = jnp.stack([key.astype(jnp.bfloat16), value.astype(jnp.bfloat16)])
    widened = extended(stacked, (("seq", 1),), rows)
    seg_keys = segment_at(ends, first - rows + jnp.arange(3 * rows, dtype=jnp.int32))
    keys_all = widened[0].reshape(3 * rows, H, HD)
    values_all = widened[1].reshape(3 * rows, H, HD)
    block = min(rows, 512)
    scale = 1.0 / HD**0.5

    def one_block(pair):
        q_blk, seg_q = pair
        score = (
            jnp.einsum(
                "qhd,khd->hqk",
                q_blk.reshape(block, H, HD),
                keys_all,
                preferred_element_type=jnp.float32,
            )
            * scale
        )
        score = jnp.where((seg_q[:, None] == seg_keys[None, :])[None], score, -1e30)
        top = jnp.max(score, axis=-1, keepdims=True)
        expo = jnp.exp(score - top)
        weights = (expo / jnp.sum(expo, axis=-1, keepdims=True)).astype(jnp.bfloat16)
        ctx = jnp.einsum("hqk,khd->qhd", weights, values_all, preferred_element_type=jnp.float32)
        return ctx.astype(jnp.bfloat16).reshape(block, H * HD)

    context = lax.map(
        one_block,
        (query.reshape(rows // block, block, H * HD), seg_own.reshape(rows // block, block)),
    ).reshape(rows, H * HD)
    attn = add_rows(context, unpack(g, 3, True))
    after_attn = (frames.astype(jnp.float32) + attn).astype(jnp.bfloat16)
    conv_in = layer_norm(after_attn.astype(jnp.float32), norm_conv).astype(jnp.bfloat16)
    channels = kernel.shape[1]
    expanded = add_rows(conv_in, jnp.concatenate([unpack(g, 4, False), unpack(g, 5, False)], axis=1))
    glu = (expanded[:, :channels] * jax.nn.sigmoid(expanded[:, channels:])).astype(jnp.bfloat16)
    glu_rim = extended(glu, (("seq", 0),), half)
    seg_rim = segment_at(ends, first - half + jnp.arange(rows + 2 * half, dtype=jnp.int32))
    depth = depthwise(glu_rim, seg_rim, seg_own, kernel, rows)
    moved = depth * bn_gain + bn_bias
    activated = (moved * jax.nn.sigmoid(moved)).astype(jnp.bfloat16)
    shrunk = add_rows(activated, unpack(g, 6, True))
    block_out = layer_norm(after_attn.astype(jnp.float32) + shrunk, norm_final).astype(jnp.bfloat16)
    recordings = lengths.shape[0]
    member = (seg_own[:, None] == jnp.arange(recordings, dtype=jnp.int32)[None, :]).astype(
        jnp.bfloat16
    )
    partial_sums = lax.dot_general(
        member, block_out, (((0,), (0,)), ((), ())), preferred_element_type=jnp.float32
    )
    sums = lax.psum(partial_sums, "seq")
    pooled = sums / lengths.astype(jnp.float32)[:, None]
    return (block_out, pooled)


def solution(mesh):
    return jax.shard_map(
        local,
        mesh=mesh,
        in_specs=(
            P(("rep", "seq"), None),
            P("rep"),
            P(),
            P("seq", None),
            P("seq", None),
            P("seq", None),
            P("seq", None),
            P(),
            P("seq", None),
            P(),
            P(),
            P(),
            P("seq", None),
            P(),
        ),
        out_specs=(P(("rep", "seq"), None), P("rep", None)),
        check_vma=False,
    )
```

```python
import jax
import jax.numpy as jnp
from jax import lax
from jax.experimental import pallas as pl
from jax.experimental.pallas import tpu as pltpu
from jax.sharding import PartitionSpec as P

H = 8
HD = 96
KERNEL = 31
HALF = 15
MESH = pl.DeviceIdType.MESH
F32 = jnp.float32
BF16 = jnp.bfloat16
NZ, NX, NY = 8, 4, 4
ROWS = 256
D = 1536
CH = 768
NREC = 128
UNIT = 1152
COLS = 7 * UNIT
GROUPS = ((0, 2, (6, 8, 4)), (2, 4, (5, 5, 8)), (4, 6, (5, 5, 8)), (6, 7, (3, 2, 4)))
N_COPIES = 330


class Place:
    def __init__(self):
        self.index = lax.axis_index("seq")
        self.z = self.index // 8
        self.x = (self.index // 2) % 4
        self.c = self.index % 2
        self.y = lax.axis_index("rep")

    def at(self, dz=0, dx=0, dc=0, dy=0):
        z = (self.z + dz + NZ) % NZ
        x = (self.x + dx + NX) % NX
        c = (self.c + dc) % 2
        y = (self.y + dy + NY) % NY
        return {"seq": z * 8 + x * 2 + c, "rep": y}

    def beside(self, step):
        return {"seq": (self.index + step + 64) % 64, "rep": self.y}

    def partners(self):
        found = [self.at(dz=k) for k in range(1, NZ)]
        found += [self.at(dx=k) for k in range(1, NX)]
        found += [self.at(dy=1), self.at(dy=-1), self.at(dc=1), self.beside(2 * self.c - 1)]
        return found


class Copies:
    def __init__(self, send_sem, recv_sem):
        self.send_sem, self.recv_sem = send_sem, recv_sem
        self.all = []

    def send(self, src, dst, device):
        k = len(self.all)
        copy = pltpu.make_async_remote_copy(
            src_ref=src,
            dst_ref=dst,
            send_sem=self.send_sem.at[k],
            recv_sem=self.recv_sem.at[k],
            device_id=device,
            device_id_type=MESH,
        )
        copy.start()
        self.all.append(copy)
        return copy

    def finish(self):
        for copy in self.all:
            copy.wait_send()


class Gather:
    def __init__(self, copies, place, ref, own):
        self.copies, self.place, self.ref, self.own = copies, place, ref, own

    def push(self, region, device):
        part = self.ref.at[region]
        return self.copies.send(part, part, device)

    def ring(self, axis, region, shared):
        place = self.place
        n = {"z": NZ, "x": NX, "y": NY}[axis]
        me = {"z": place.z, "x": place.x, "y": place.y}[axis]
        up, down, other = place.at(**{"d" + axis: 1}), place.at(**{"d" + axis: -1}), place.at(dc=1)
        forth = self.push(region(me, None), up)
        back = self.push(region(me, None), down)
        for step in range(1, n // 2):
            low, high = (me - step + n) % n, (me + step) % n
            last = step == n // 2 - 1
            yield
            forth.wait_recv()
            forth = self.push(region(low, 0 if last else None), up)
            back.wait_recv()
            rest = region(high, 1 if last else None)
            back = None if rest is None else self.push(rest, down)
            shared.append(self.push(region(low, None), other))
            shared.append(self.push(region(high, None), other))
        yield
        forth.wait_recv()
        if back is not None:
            back.wait_recv()
        shared.append(self.push(region((me + n // 2) % n, None), other))

    def part(self, order, lo, tiles, shared):
        place = self.place
        quarter = tiles // 4 if "y" in order else tiles

        def cut(k, half, count):
            start, size = 0, count * 128
            if half is not None:
                first = (count + 1) // 2 * 128
                start, size = (0, first) if half == 0 else (first, size - first)
            if "y" not in order:
                return pl.ds(lo + start, size)
            return pl.ds(pl.multiple_of(lo + k * (quarter * 128) + start, 128), size)

        done = set()
        for axis in order:

            def region(k, half, axis=axis, done=frozenset(done)):
                at = {"z": place.z, "x": place.x, "y": place.y}
                at[axis] = k
                z = slice(None) if "z" in done else at["z"]
                x = slice(None) if "x" in done else at["x"]
                if half is not None and quarter == 1:
                    if axis == "x":
                        z = pl.ds(half * (NZ // 2), NZ // 2) if "z" in done else z
                    elif axis == "y":
                        z = pl.ds(half * (NZ // 2), NZ // 2)
                    elif half == 1:
                        return None
                    half = None
                return (z, x, place.c, slice(None), cut(at["y"], half, quarter))

            yield from self.ring(axis, region, shared)
            done.add(axis)

    def start(self, group):
        place = self.place
        first, end, tiles = GROUPS[group]
        lo, hi = first * UNIT, end * UNIT
        quarter = tiles[2] * 32
        mid = hi - 4 * quarter
        shared = []
        for cols in (pl.ds(lo, mid - lo), pl.ds(pl.multiple_of(mid + place.y * quarter, 128), quarter)):
            region = (place.z, place.x, place.c, slice(None), cols)
            self.ref[region] = self.own[:, cols]
            shared.append(self.push(region, place.at(dc=1)))
        parts = []
        for order, count in zip(("xz", "zx", "zxy"), tiles):
            if count:
                parts.append(self.part(order, lo, count, shared))
                lo += count * 128
        return Group(parts, shared)


class Group:
    def __init__(self, parts, shared):
        self.parts, self.shared = parts, shared
        self.round()

    def round(self, count=1):
        for _ in range(count):
            self.parts = [part for part in self.parts if next(part, True) is None]

    def finish(self):
        while self.parts:
            self.round()
        for copy in self.shared:
            copy.wait_recv()


def fold(rows8):
    half = rows8.shape[1] // 2
    return jnp.concatenate([rows8[:, :half], rows8[:, half:]], axis=0)


def pack_own(own_ref, unit, value, first):
    main = jnp.where(first, value[:16], value[8:])
    rest = jnp.where(first, value[16:], value[:8])
    whole = jnp.concatenate([main, fold(rest)], axis=1).astype(BF16)
    own_ref[:, unit * UNIT : (unit + 1) * UNIT] = whole


def unfold(low, high):
    low, high = low.astype(F32), high.astype(F32)
    left = jnp.concatenate([low[:8], high[:8]], axis=0)
    right = jnp.concatenate([low[8:], high[8:]], axis=0)
    return jnp.concatenate([left, right], axis=1).astype(BF16)


def lay_rows(g_ref, unit, w_ref, column):
    lo = unit * UNIT

    @pl.loop(0, NZ)
    def _(z):
        for x in range(NX):
            row = z * 192 + x * 48
            low, high = g_ref[z, x, 0, :, lo : lo + UNIT], g_ref[z, x, 1, :, lo : lo + UNIT]
            for k, value in enumerate((low[:, :CH], unfold(low[:, CH:], high[:, CH:]), high[:, :CH])):
                w_ref[pl.ds(pl.multiple_of(row + 16 * k, 16), 16), column : column + CH] = value


def lay_halves(g_ref, unit, w_ref):
    lo = unit * UNIT

    @pl.loop(0, NZ)
    def _(z):
        for pair in range(2):
            for c in range(2):
                row = z * 96 + pair * 48
                low = g_ref[z, 2 * pair, c, :, lo : lo + UNIT]
                high = g_ref[z, 2 * pair + 1, c, :, lo : lo + UNIT]
                for k, value in enumerate((low[:, :CH], unfold(low[:, CH:], high[:, CH:]), high[:, :CH])):
                    w_ref[pl.ds(pl.multiple_of(row + 16 * k, 16), 16), c * CH : (c + 1) * CH] = value


def norm_rows(values, gain):
    mean = jnp.mean(values, axis=-1, keepdims=True)
    centred = values - mean
    var = jnp.mean(centred * centred, axis=-1, keepdims=True)
    return centred * lax.rsqrt(var + 1e-05) * gain


def norm_into(src, gain, dst):
    @pl.loop(0, ROWS // 32)
    def _(i):
        rows = pl.ds(pl.multiple_of(i * 32, 32), 32)
        dst[rows, :] = norm_rows(src[rows, :].astype(F32), gain[...]).astype(BF16)


def times(x_ref, w_ref, column):
    return jnp.dot(
        x_ref[...], w_ref[:, pl.ds(pl.multiple_of(column, 256), 256)], preferred_element_type=F32
    )


def bounds(len_ref, place, bound_ref, member_ref, inverse_ref):
    lengths = len_ref[...].astype(F32)
    row = lax.broadcasted_iota(jnp.int32, (NREC, NREC), 0)
    col = lax.broadcasted_iota(jnp.int32, (NREC, NREC), 1)
    before = (row <= col).astype(BF16)
    wide = jnp.broadcast_to(lengths, (NREC, NREC))
    ends = jnp.dot(wide.astype(BF16), before, preferred_element_type=F32)
    first = (place.index * ROWS).astype(F32)
    t = lax.broadcasted_iota(jnp.int32, (ROWS, NREC), 0).astype(F32) + first
    end_row = jnp.broadcast_to(ends[:1], (ROWS, NREC))
    begin = jnp.max(jnp.where(end_row <= t, end_row, 0.0), axis=1, keepdims=True)
    finish = jnp.min(jnp.where(end_row > t, end_row, 65536.0), axis=1, keepdims=True)
    bound_ref[0] = jnp.broadcast_to(begin, (ROWS, NREC)) - t
    bound_ref[1] = jnp.broadcast_to(finish, (ROWS, NREC)) - t
    eye = row == col
    end_col = jnp.sum(jnp.where(eye, ends, 0.0), axis=1, keepdims=True)
    len_col = jnp.sum(jnp.where(eye, wide, 0.0), axis=1, keepdims=True)
    inverse_ref[...] = jnp.broadcast_to(1.0 / len_col, (NREC, NREC))
    at = lax.broadcasted_iota(jnp.int32, (NREC, ROWS), 1).astype(F32) + first
    inside = (at < end_col) & (at >= end_col - len_col)
    member_ref[...] = inside.astype(F32).astype(BF16)


def attend(q_ref, kv_ref, bound_ref, ctx_ref):
    factor = 1.4426950408889634 / HD**0.5
    span = 640

    @pl.loop(0, 4)
    def _(i):
        top, lane0 = (i // 2) * 128, (i % 2) * 384
        rows = pl.ds(pl.multiple_of(top, 128), 128)
        window = pl.ds(pl.multiple_of(top, 128), span)
        offset = lax.broadcasted_iota(jnp.int32, (128, span), 1) - lax.broadcasted_iota(jnp.int32, (128, span), 0)
        offset = (offset - ROWS).astype(F32)
        inside = (offset >= bound_ref[0, rows, :1]) & (offset < bound_ref[1, rows, :1])
        bias = jnp.where(inside, 0.0, -1e30)
        outs = []
        for h in range(4):
            lo, hi = h * HD, (h + 1) * HD
            a, b = lo // 128 * 128, (hi + 127) // 128 * 128
            lane = lax.broadcasted_iota(jnp.int32, (128, b - a), 1) + a
            cols = pl.ds(pl.multiple_of(lane0 + a, 128), b - a)
            q = q_ref[rows, cols]
            q = jnp.where((lane >= lo) & (lane < hi), q.astype(F32), 0.0).astype(BF16)
            score = lax.dot_general(
                q, kv_ref[window, cols], (((1,), (1,)), ((), ())), preferred_element_type=F32
            )
            score = score + bias
            peak = jnp.max(score, axis=1, keepdims=True)
            expo = jnp.exp2((score - peak) * factor)
            total = jnp.sum(expo, axis=1, keepdims=True)
            values = kv_ref[window, pl.ds(pl.multiple_of(CH + lane0 + a, 128), b - a)]
            out = jnp.dot(expo.astype(BF16), values, preferred_element_type=F32)
            outs.append((a, out / total))
        for tile in range(3):
            lane = lax.broadcasted_iota(jnp.int32, (128, 128), 1)
            at = tile * 128
            one, two = outs[tile], outs[tile + 1]
            left = one[1][:, at - one[0] : at - one[0] + 128]
            right = two[1][:, at - two[0] : at - two[0] + 128]
            whole = jnp.where(lane < (tile + 1) * HD - at, left, right).astype(BF16)
            ctx_ref[rows, pl.ds(pl.multiple_of(lane0 + at, 128), 128)] = whole


def convolve(first, count, glu_ref, bound_ref, taps, gain, bias, act_ref):
    @pl.loop(0, count)
    def _(i):
        top = pl.multiple_of((i + first) * 32, 32)
        rows = pl.ds(top, 32)
        behind, ahead = bound_ref[0, rows, :], bound_ref[1, rows, :]
        for tile in range(CH // 128):
            lanes = slice(tile * 128, (tile + 1) * 128)
            depth = jnp.zeros((32, 128), F32)
            for j in range(KERNEL):
                source = glu_ref[tile, pl.ds(top + j + 1, 32), :]
                if j < HALF:
                    source = jnp.where(behind <= float(j - HALF), source, 0.0)
                elif j > HALF:
                    source = jnp.where(ahead > float(j - HALF), source, 0.0)
                depth = depth + taps[j : j + 1, lanes] * source
            moved = depth * gain[:, lanes] + bias[:, lanes]
            act_ref[rows, lanes] = (moved * jax.nn.sigmoid(moved)).astype(BF16)


def pool(copies, place, part_ref, give, take, sum_ref, sum16, rx, s2, rz, zb, xb, sb, out_ref):
    c = place.c
    copy = copies.send(give.at[1 - c], take, place.at(dc=1))
    copy.wait_recv()
    sum_ref[...] = part_ref[c] + take[...].astype(F32)
    sum16[...] = sum_ref[...].astype(BF16)
    got = []
    for k in range(1, NX):
        rows = pl.ds(pl.multiple_of((place.x + k) % NX * 32, 32), 32)
        got.append(copies.send(sum16.at[rows], rx.at[k - 1], place.at(dx=k)))
    total = sum_ref[pl.ds(pl.multiple_of(place.x * 32, 32), 32), :]
    for k, copy in enumerate(got):
        copy.wait_recv()
        total = total + rx[k].astype(F32)
    for j in range(NZ):
        s2[j] = total[8 * (j // 2) : 8 * (j // 2) + 8, 384 * (j % 2) : 384 * (j % 2) + 384]
    got = [copies.send(s2.at[(place.z + k) % NZ], rz.at[k - 1], place.at(dz=k)) for k in range(1, NZ)]
    total = s2[place.z]
    for k, copy in enumerate(got):
        copy.wait_recv()
        total = total + rz[k]
    zb[place.z] = total
    got = [copies.send(zb.at[place.z], zb.at[place.z], place.at(dz=k)) for k in range(1, NZ)]
    for copy in got:
        copy.wait_recv()
    parts = [jnp.concatenate([zb[2 * j], zb[2 * j + 1]], axis=1) for j in range(4)]
    xb[place.x] = jnp.concatenate(parts, axis=0).astype(BF16)
    got = [copies.send(xb.at[place.x], xb.at[place.x], place.at(dx=k)) for k in range(1, NX)]
    for copy in got:
        copy.wait_recv()
    copies.send(xb, sb, place.at(dc=1)).wait_recv()
    for k in range(NX):
        mine, theirs = xb[k].astype(F32), sb[k].astype(F32)
        out_ref[32 * k : 32 * k + 32, :CH] = jnp.where(c == 0, mine, theirs)
        out_ref[32 * k : 32 * k + 32, CH:] = jnp.where(c == 0, theirs, mine)


def block_kernel(
    frames, lengths, g_attn, wq, wk, wv, wo, g_conv, we, taps, bn_gain, bn_bias, ws, g_final,
    out_ref, pooled_ref,
    g_ref, own_ref, w_kv, w_q, w_o, w_e, w_s, give, take, normed, query, kv, ctx, after, glu16, glu_ref, rim, act, moved,
    bound_ref, member_ref, inverse_ref, part_ref, pool_give, pool_take, sum_ref, sum16, rx, s2, rz, zb, xb, sb,
    send_sem, recv_sem,
):
    place = Place()
    barrier = pltpu.get_barrier_semaphore()
    partners = place.partners()
    for partner in partners:
        pl.semaphore_signal(barrier, inc=1, device_id=partner, device_id_type=MESH)
    lead = place.c == 0
    pack_own(own_ref, 0, wk[...].astype(F32), lead)
    pack_own(own_ref, 1, wv[...].astype(F32), lead)
    for k, ref in enumerate((wo, ws)):
        value = ref[...].astype(F32)
        theirs = jnp.where(lead, value[:, CH:], value[:, :CH])
        give[k] = jnp.concatenate([theirs, jnp.zeros((4, CH), F32)], axis=0).astype(BF16)
    pl.semaphore_wait(barrier, len(partners))

    copies = Copies(send_sem, recv_sem)
    gather = Gather(copies, place, g_ref, own_ref)
    g0 = gather.start(0)
    side = copies.send(give, take, place.at(dc=1))
    pack_own(own_ref, 2, wq[...].astype(F32), lead)
    pack_own(own_ref, 4, we[:, :CH].astype(F32), lead)
    pack_own(own_ref, 5, we[:, CH:].astype(F32), lead)
    g0.round()
    side.wait_recv()
    for k, (unit, ref) in enumerate(((3, wo), (6, ws))):
        value = ref[...].astype(F32)
        own = jnp.where(lead, value[:, :CH], value[:, CH:])
        got = take[k].astype(F32)[:12]
        both = jnp.where(lead, jnp.concatenate([own, got], axis=0), jnp.concatenate([got, own], axis=0))
        pack_own(own_ref, unit, both, place.x % 2 == 0)
    g0.round()
    g1 = gather.start(1)
    bounds(lengths, place, bound_ref, member_ref, inverse_ref)
    g0.round()
    g1.round()
    norm_into(frames, g_attn, normed)
    g0.round()
    g1.round()
    g2 = gather.start(2)
    g0.round()
    g1.round()
    g2.round()
    g0.round()
    g1.round()
    g2.round()
    g3 = gather.start(3)
    g0.round()
    g1.round()
    g2.round()
    g3.round()
    g0.finish()
    lay_rows(g_ref, 0, w_kv, 0)
    lay_rows(g_ref, 1, w_kv, CH)
    g1.round()
    g2.round()
    g3.round()

    @pl.loop(0, 6)
    def _(n):
        kv[ROWS : 2 * ROWS, pl.ds(pl.multiple_of(n * 256, 256), 256)] = times(normed, w_kv, n * 256).astype(BF16)

    own = kv.at[pl.ds(ROWS, ROWS)]
    to_left = copies.send(own, kv.at[pl.ds(2 * ROWS, ROWS)], place.beside(-1))
    to_right = copies.send(own, kv.at[pl.ds(0, ROWS)], place.beside(1))
    g1.round()
    g2.round()
    g3.round()
    g1.finish()
    lay_rows(g_ref, 2, w_q, 0)

    @pl.loop(0, 3)
    def _(n):
        query[:, pl.ds(pl.multiple_of(n * 256, 256), 256)] = times(normed, w_q, n * 256).astype(BF16)

    g2.round()
    g3.round()
    lay_halves(g_ref, 3, w_o)
    g2.round()
    g3.round()
    to_left.wait_recv()
    to_right.wait_recv()
    attend(query, kv, bound_ref, ctx)
    g2.round()
    g3.round()

    @pl.loop(0, 6)
    def _(n):
        cols = pl.ds(pl.multiple_of(n * 256, 256), 256)
        after[:, cols] = (frames[:, cols].astype(F32) + times(ctx, w_o, n * 256)).astype(BF16)

    norm_into(after, g_conv, normed)
    g2.finish()
    g3.round()
    lay_rows(g_ref, 4, w_e, 0)
    lay_rows(g_ref, 5, w_e, CH)

    for n in range(3):
        gate = times(normed, w_e, CH + n * 256)
        value = times(normed, w_e, n * 256)
        glu = (value * jax.nn.sigmoid(gate)).astype(BF16)
        glu16[:, n * 256 : n * 256 + 256] = glu
        wide = glu.astype(F32)
        glu_ref[2 * n, 16 : 16 + ROWS, :] = wide[:, :128]
        glu_ref[2 * n + 1, 16 : 16 + ROWS, :] = wide[:, 128:]
    rim_left = copies.send(glu16.at[pl.ds(0, 16)], rim.at[1], place.beside(-1))
    rim_right = copies.send(glu16.at[pl.ds(ROWS - 16, 16)], rim.at[0], place.beside(1))
    g3.finish()
    lay_halves(g_ref, 6, w_s)
    convolve(1, 6, glu_ref, bound_ref, taps, bn_gain, bn_bias, act)
    rim_left.wait_recv()
    rim_right.wait_recv()
    for tile in range(CH // 128):
        lanes = slice(tile * 128, (tile + 1) * 128)
        glu_ref[tile, :16, :] = rim[0, :, lanes].astype(F32)
        glu_ref[tile, 16 + ROWS :, :] = rim[1, :, lanes].astype(F32)
    convolve(0, 1, glu_ref, bound_ref, taps, bn_gain, bn_bias, act)
    convolve(7, 1, glu_ref, bound_ref, taps, bn_gain, bn_bias, act)

    @pl.loop(0, 6)
    def _(n):
        cols = pl.ds(pl.multiple_of(n * 256, 256), 256)
        moved[:, cols] = after[:, cols].astype(F32) + times(act, w_s, n * 256)

    norm_into(moved, g_final, out_ref)
    for h in range(2):
        for n in range(3):
            cols = slice(h * CH + n * 256, h * CH + n * 256 + 256)
            sums = jnp.dot(member_ref[...], out_ref[:, cols], preferred_element_type=F32) * inverse_ref[:, :1]
            part_ref[h, :, n * 256 : n * 256 + 256] = sums
            pool_give[h, :, n * 256 : n * 256 + 256] = sums.astype(BF16)
    pool(copies, place, part_ref, pool_give, pool_take, sum_ref, sum16, rx, s2, rz, zb, xb, sb, pooled_ref)
    copies.finish()


def local(frames, lengths, norm_attn, w_query, w_key, w_value, w_out, norm_conv, w_expand, kernel, bn_gain,
          bn_bias, w_shrink, norm_final):
    vmem = pl.BlockSpec(memory_space=pltpu.VMEM)
    return tuple(
        pl.pallas_call(
            block_kernel,
            out_shape=[
                jax.ShapeDtypeStruct((ROWS, D), BF16),
                jax.ShapeDtypeStruct((NREC, D), F32),
            ],
            in_specs=[vmem] * 14,
            out_specs=[vmem] * 2,
            scratch_shapes=[
                pltpu.VMEM((NZ, NX, 2, 16, COLS), BF16),
                pltpu.VMEM((16, COLS), BF16),
                pltpu.VMEM((D, 2 * CH), BF16),
                pltpu.VMEM((D, CH), BF16),
                pltpu.VMEM((CH, D), BF16),
                pltpu.VMEM((D, 2 * CH), BF16),
                pltpu.VMEM((CH, D), BF16),
                pltpu.VMEM((2, 16, CH), BF16),
                pltpu.VMEM((2, 16, CH), BF16),
                pltpu.VMEM((ROWS, D), BF16),
                pltpu.VMEM((ROWS, CH), BF16),
                pltpu.VMEM((3 * ROWS, 2 * CH), BF16),
                pltpu.VMEM((ROWS, CH), BF16),
                pltpu.VMEM((ROWS, D), BF16),
                pltpu.VMEM((ROWS, CH), BF16),
                pltpu.VMEM((CH // 128, ROWS + 32, 128), F32),
                pltpu.VMEM((2, 16, CH), BF16),
                pltpu.VMEM((ROWS, CH), BF16),
                pltpu.VMEM((ROWS, D), F32),
                pltpu.VMEM((2, ROWS, NREC), F32),
                pltpu.VMEM((NREC, ROWS), BF16),
                pltpu.VMEM((NREC, NREC), F32),
                pltpu.VMEM((2, NREC, CH), F32),
                pltpu.VMEM((2, NREC, CH), BF16),
                pltpu.VMEM((NREC, CH), BF16),
                pltpu.VMEM((NREC, CH), F32),
                pltpu.VMEM((NREC, CH), BF16),
                pltpu.VMEM((NX - 1, 32, CH), BF16),
                pltpu.VMEM((NZ, 8, 384), F32),
                pltpu.VMEM((NZ - 1, 8, 384), F32),
                pltpu.VMEM((NZ, 8, 384), F32),
                pltpu.VMEM((NX, 32, CH), BF16),
                pltpu.VMEM((NX, 32, CH), BF16),
                pltpu.SemaphoreType.DMA((N_COPIES,)),
                pltpu.SemaphoreType.DMA((N_COPIES,)),
            ],
            compiler_params=pltpu.CompilerParams(
                collective_id=0, has_side_effects=True, vmem_limit_bytes=60 << 20
            ),
            cost_estimate=pl.CostEstimate(flops=5_000_000_000, bytes_accessed=20_000_000, transcendentals=3_000_000),
        )(
            frames, lengths.reshape(1, NREC), norm_attn.reshape(1, D), w_query, w_key, w_value, w_out,
            norm_conv.reshape(1, D), w_expand, kernel, bn_gain.reshape(1, CH), bn_bias.reshape(1, CH), w_shrink,
            norm_final.reshape(1, D),
        )
    )


def solution(mesh):
    return jax.shard_map(
        local,
        mesh=mesh,
        in_specs=(
            P(("rep", "seq"), None),
            P("rep"),
            P(),
            P("seq", None),
            P("seq", None),
            P("seq", None),
            P("seq", None),
            P(),
            P("seq", None),
            P(),
            P(),
            P(),
            P("seq", None),
            P(),
        ),
        out_specs=(P(("rep", "seq"), None), P("rep", None)),
        check_vma=False,
    )
```

```python
import jax
import jax.numpy as jnp
from jax import lax
from jax.experimental import pallas as pl
from jax.experimental.pallas import tpu as pltpu
from jax.sharding import PartitionSpec as P

H = 8
HD = 96
KERNEL = 31
HALF = 15
MESH = pl.DeviceIdType.MESH
F32 = jnp.float32
BF16 = jnp.bfloat16
NZ, NX, NY = 8, 4, 4
ROWS = 256
D = 1536
CH = 768
NREC = 128
UNIT = 1152
COLS = 7 * UNIT
GROUPS = (
    (0, 2, (7, 7, 4), ('straight', 'ring', 'ring', 'ring', 'straight')),
    (2, 4, (7, 3, 8), ('straight', 'ring', 'ring', 'ring', 'hops')),
    (4, 6, (5, 5, 8), ('ring', 'ring', 'ring', 'ring', 'straight')),
    (6, 7, (1, 0, 8), ('straight', 'ring', 'hops', 'ring', 'ring')),
)
N_COPIES = 112
PLAN = (
    "start0", "sendfr", "packrest", "bounds", "packos", "01", "start1", "00", "02", "start3", "norma",
    "normb", "01", "11", "12", "start2", "00", "32", "01", "11", "12", "21", "normx", "normy", "10", "22",
    "02", "30", "20", "00", "32", "01", "11", "21", "12", "22", "10", "20", "30", "02", "00", "32", "11",
    "21", "10", "12", "20", "02", "30", "01", "00", "32", "22", "21", "laykv", "12", "10", "mmkv0", "11",
    "20", "mmkv1", "10", "32", "sendkv", "layq", "mmq", "22", "20", "layo", "21", "att0", "att1", "att2",
    "20", "att3", "21", "32", "mmo", "normc", "22", "normd", "laye", "mme0", "mme1", "32", "mme2", "sendrim",
    "conv0", "conv1", "lays", "conv2", "mms", "fin",
)


class Place:
    def __init__(self):
        self.index = lax.axis_index("seq")
        self.z = self.index // 8
        self.x = (self.index // 2) % 4
        self.c = self.index % 2
        self.y = lax.axis_index("rep")

    def at(self, dz=0, dx=0, dc=0, dy=0):
        z = (self.z + dz + NZ) % NZ
        x = (self.x + dx + NX) % NX
        c = (self.c + dc) % 2
        y = (self.y + dy + NY) % NY
        return {"seq": z * 8 + x * 2 + c, "rep": y}

    def beside(self, step):
        return {"seq": (self.index + step + 64) % 64, "rep": self.y}

    def partners(self):
        found = [self.at(dz=k) for k in range(1, NZ)]
        found += [self.at(dx=k) for k in range(1, NX)]
        found += [self.at(dy=k) for k in range(1, NY)]
        found += [self.at(dc=1), self.beside(2 * self.c - 1)]
        return found


class Copies:
    def __init__(self, send_sem, recv_sem):
        self.send_sem, self.recv_sem = send_sem, recv_sem
        self.count = 0
        self.all = []

    def sems(self):
        self.count += 1
        return {"send_sem": self.send_sem.at[self.count - 1], "recv_sem": self.recv_sem.at[self.count - 1]}

    def send(self, src, dst, device):
        copy = pltpu.make_async_remote_copy(
            src_ref=src, dst_ref=dst, device_id=device, device_id_type=MESH, **self.sems()
        )
        copy.start()
        self.all.append(copy)
        return copy

    def finish(self):
        for copy in self.all:
            copy.wait_send()


class Batch:
    def __init__(self, copies, ref, whole, device):
        self.ref, self.sems = ref, copies.sems()
        self.total = self.make(whole, device)
        copies.all.append(self)

    def make(self, region, device):
        part = self.ref.at[region]
        return pltpu.make_async_remote_copy(
            src_ref=part, dst_ref=part, device_id=device, device_id_type=MESH, **self.sems
        )

    def push(self, region, device):
        self.make(region, device).start()

    def wait_recv(self):
        self.total.wait_recv()

    def wait_send(self):
        self.total.wait_send()


class Gather:
    def __init__(self, copies, place, ref, own):
        self.copies, self.place, self.ref, self.own = copies, place, ref, own

    def batch(self, whole):
        return Batch(self.copies, self.ref, whole, self.place.at(dc=1))

    def straight(self, axis, n, region, many, shared):
        place = self.place
        me = {"z": place.z, "x": place.x, "y": place.y}[axis]
        sent = self.batch(many(n - 1))
        for k in range(1, n):
            sent.push(region(me, None), place.at(**{"d" + axis: k}))
        yield
        sent.wait_recv()
        for k in range(1, n):
            shared.push(region((me - k + n) % n, None), place.at(dc=1))

    def hops(self, region, many, shared):
        place = self.place
        me, other = place.z, place.at(dc=1)
        block = lambda k: region((me + k + NZ) % NZ, None)
        sent = self.batch(many(4))
        for k in (1, -1, 2, -2):
            sent.push(block(0), place.at(dz=k))
        yield
        sent.wait_recv()
        sent = self.batch(many(3))
        for k in (1, -1):
            sent.push(block(-2 * k), place.at(dz=k))
        for k in (1, -1):
            half = region((me - 2 * k + NZ) % NZ, 0 if k == 1 else 1)
            if half is not None:
                sent.push(half, place.at(dz=2 * k))
        for k in (1, -1, 2, -2):
            shared.push(block(k), other)
        yield
        sent.wait_recv()
        for k in (3, -3, 4):
            shared.push(block(k), other)

    def ring(self, axis, region, many, shared):
        place = self.place
        n = {"z": NZ, "x": NX, "y": NY}[axis]
        me = {"z": place.z, "x": place.x, "y": place.y}[axis]
        up, down, other = place.at(**{"d" + axis: 1}), place.at(**{"d" + axis: -1}), place.at(dc=1)
        sent = self.batch(many(2))
        sent.push(region(me, None), up)
        sent.push(region(me, None), down)
        for step in range(1, n // 2):
            low, high = (me - step + n) % n, (me + step) % n
            last = step == n // 2 - 1
            yield
            sent.wait_recv()
            sent = self.batch(many(1 if last else 2))
            sent.push(region(low, 0 if last else None), up)
            rest = region(high, 1 if last else None)
            if rest is not None:
                sent.push(rest, down)
            shared.push(region(low, None), other)
            shared.push(region(high, None), other)
        yield
        sent.wait_recv()
        shared.push(region((me + n // 2) % n, None), other)

    def part(self, order, lo, tiles, modes, shared):
        place = self.place
        quarter = tiles // 4 if "y" in order else tiles

        def cut(k, half, count):
            start, size = 0, count * 128
            if half is not None:
                first = (count + 1) // 2 * 128
                start, size = (0, first) if half == 0 else (first, size - first)
            if "y" not in order:
                return pl.ds(lo + start, size)
            return pl.ds(pl.multiple_of(lo + k * (quarter * 128) + start, 128), size)

        done = set()
        for axis in order:

            def region(k, half, axis=axis, done=frozenset(done)):
                at = {"z": place.z, "x": place.x, "y": place.y}
                at[axis] = k
                z = slice(None) if "z" in done else at["z"]
                x = slice(None) if "x" in done else at["x"]
                if half == 1 and quarter == 1:
                    return None
                return (z, x, place.c, slice(None), cut(at["y"], half, quarter))

            def many(count, axis=axis, region=region):
                at = list(region({"z": place.z, "x": place.x, "y": place.y}[axis], None))
                if axis == "y":
                    at[4] = pl.ds(lo, count * quarter * 128)
                else:
                    at["zx".index(axis)] = pl.ds(0, count)
                return tuple(at)

            mode = modes[axis]
            if mode == "hops":
                yield from self.hops(region, many, shared)
            elif mode == "ring":
                yield from self.ring(axis, region, many, shared)
            else:
                yield from self.straight(axis, {"z": NZ, "x": NX, "y": NY}[axis], region, many, shared)
            done.add(axis)

    def start(self, group):
        place = self.place
        first, end, tiles, ways = GROUPS[group]
        lo, hi = first * UNIT, end * UNIT
        quarter = tiles[2] * 32
        mid = hi - 4 * quarter
        shared = self.batch((slice(None), slice(None), place.c, slice(None), pl.ds(lo, hi - lo)))
        spans = []
        if mid > lo:
            spans.append(pl.ds(lo, mid - lo))
        if quarter:
            spans.append(pl.ds(pl.multiple_of(mid + place.y * quarter, 128), quarter))
        for cols in spans:
            region = (place.z, place.x, place.c, slice(None), cols)
            self.ref[region] = self.own[:, cols]
            shared.push(region, place.at(dc=1))
        parts = {}
        for k, (order, count) in enumerate(zip(("xz", "zx", "zxy"), tiles)):
            if count:
                parts[k] = self.part(order, lo, count, {"x": ways[0], "y": ways[1], "z": ways[2 + k]}, shared)
                lo += count * 128
        return Group(parts, shared)


class Group:
    def __init__(self, parts, shared):
        self.parts, self.shared = parts, shared
        for part in parts.values():
            next(part)

    def step(self, k):
        if next(self.parts[k], True) is not None:
            del self.parts[k]

    def finish(self):
        if self.shared is not None:
            self.shared.wait_recv()
        self.shared = None
        return not self.parts


def fold(rows8):
    half = rows8.shape[1] // 2
    return jnp.concatenate([rows8[:, :half], rows8[:, half:]], axis=0)


def pack_own(own_ref, unit, value, first):
    main = jnp.where(first, value[:16], value[8:])
    rest = jnp.where(first, value[16:], value[:8])
    whole = jnp.concatenate([main, fold(rest)], axis=1).astype(BF16)
    own_ref[:, unit * UNIT : (unit + 1) * UNIT] = whole


def unfold(low, high):
    low, high = low.astype(F32), high.astype(F32)
    left = jnp.concatenate([low[:8], high[:8]], axis=0)
    right = jnp.concatenate([low[8:], high[8:]], axis=0)
    return jnp.concatenate([left, right], axis=1).astype(BF16)


def lay_rows(g_ref, unit, w_ref, column):
    lo = unit * UNIT

    @pl.loop(0, NZ)
    def _(z):
        for x in range(NX):
            row = z * 192 + x * 48
            low, high = g_ref[z, x, 0, :, lo : lo + UNIT], g_ref[z, x, 1, :, lo : lo + UNIT]
            for k, value in enumerate((low[:, :CH], unfold(low[:, CH:], high[:, CH:]), high[:, :CH])):
                w_ref[pl.ds(pl.multiple_of(row + 16 * k, 16), 16), column : column + CH] = value


def lay_halves(g_ref, unit, w_ref):
    lo = unit * UNIT

    @pl.loop(0, NZ)
    def _(z):
        for pair in range(2):
            for c in range(2):
                row = z * 96 + pair * 48
                low = g_ref[z, 2 * pair, c, :, lo : lo + UNIT]
                high = g_ref[z, 2 * pair + 1, c, :, lo : lo + UNIT]
                for k, value in enumerate((low[:, :CH], unfold(low[:, CH:], high[:, CH:]), high[:, :CH])):
                    w_ref[pl.ds(pl.multiple_of(row + 16 * k, 16), 16), c * CH : (c + 1) * CH] = value


def norm_rows(values, gain):
    mean = jnp.mean(values, axis=-1, keepdims=True)
    centred = values - mean
    var = jnp.mean(centred * centred, axis=-1, keepdims=True)
    return centred * lax.rsqrt(var + 1e-05) * gain


def norm_into(src, gain, dst, first, end):
    @pl.loop(first, end)
    def _(i):
        rows = pl.ds(pl.multiple_of(i * 32, 32), 32)
        dst[rows, :] = norm_rows(src[rows, :].astype(F32), gain[...].reshape(1, D)).astype(BF16)


def times(x_ref, w_ref, column):
    return jnp.dot(
        x_ref[...], w_ref[:, pl.ds(pl.multiple_of(column, 256), 256)], preferred_element_type=F32
    )


def bounds(len_ref, place, bound_ref, member_ref, inverse_ref):
    lengths = len_ref[...].astype(F32)
    row = lax.broadcasted_iota(jnp.int32, (NREC, NREC), 0)
    col = lax.broadcasted_iota(jnp.int32, (NREC, NREC), 1)
    before = (row <= col).astype(BF16)
    wide = jnp.broadcast_to(lengths, (NREC, NREC))
    ends = jnp.dot(wide.astype(BF16), before, preferred_element_type=F32)
    first = (place.index * ROWS).astype(F32)
    t = lax.broadcasted_iota(jnp.int32, (ROWS, NREC), 0).astype(F32) + first
    end_row = jnp.broadcast_to(ends[:1], (ROWS, NREC))
    begin = jnp.max(jnp.where(end_row <= t, end_row, 0.0), axis=1, keepdims=True)
    finish = jnp.min(jnp.where(end_row > t, end_row, 65536.0), axis=1, keepdims=True)
    bound_ref[0] = jnp.broadcast_to(begin, (ROWS, NREC)) - t
    bound_ref[1] = jnp.broadcast_to(finish, (ROWS, NREC)) - t
    eye = row == col
    end_col = jnp.sum(jnp.where(eye, ends, 0.0), axis=1, keepdims=True)
    len_col = jnp.sum(jnp.where(eye, wide, 0.0), axis=1, keepdims=True)
    inverse_ref[...] = jnp.broadcast_to(1.0 / len_col, (NREC, NREC))
    at = lax.broadcasted_iota(jnp.int32, (NREC, ROWS), 1).astype(F32) + first
    inside = (at < end_col) & (at >= end_col - len_col)
    member_ref[...] = inside.astype(F32).astype(BF16)


def attend(i, q_ref, kv_ref, bound_ref, ctx_ref):
    factor = 1.4426950408889634 / HD**0.5
    span = 640

    top, lane0 = (i // 2) * 128, (i % 2) * 384
    rows = pl.ds(pl.multiple_of(top, 128), 128)
    window = pl.ds(pl.multiple_of(top, 128), span)
    offset = lax.broadcasted_iota(jnp.int32, (128, span), 1) - lax.broadcasted_iota(jnp.int32, (128, span), 0)
    offset = (offset - ROWS).astype(F32)
    inside = (offset >= bound_ref[0, rows, :1]) & (offset < bound_ref[1, rows, :1])
    bias = jnp.where(inside, 0.0, -1e30)
    outs = []
    for h in range(4):
        lo, hi = h * HD, (h + 1) * HD
        a, b = lo // 128 * 128, (hi + 127) // 128 * 128
        lane = lax.broadcasted_iota(jnp.int32, (128, b - a), 1) + a
        cols = pl.ds(pl.multiple_of(lane0 + a, 128), b - a)
        q = q_ref[rows, cols]
        q = jnp.where((lane >= lo) & (lane < hi), q.astype(F32), 0.0).astype(BF16)
        score = lax.dot_general(
            q, kv_ref[window, cols], (((1,), (1,)), ((), ())), preferred_element_type=F32
        )
        score = score + bias
        peak = jnp.max(score, axis=1, keepdims=True)
        expo = jnp.exp2((score - peak) * factor)
        total = jnp.sum(expo, axis=1, keepdims=True)
        values = kv_ref[window, pl.ds(pl.multiple_of(CH + lane0 + a, 128), b - a)]
        out = jnp.dot(expo.astype(BF16), values, preferred_element_type=F32)
        outs.append((a, out / total))
    for tile in range(3):
        lane = lax.broadcasted_iota(jnp.int32, (128, 128), 1)
        at = tile * 128
        one, two = outs[tile], outs[tile + 1]
        left = one[1][:, at - one[0] : at - one[0] + 128]
        right = two[1][:, at - two[0] : at - two[0] + 128]
        whole = jnp.where(lane < (tile + 1) * HD - at, left, right).astype(BF16)
        ctx_ref[rows, pl.ds(pl.multiple_of(lane0 + at, 128), 128)] = whole


def convolve(first, count, glu_ref, bound_ref, taps, gain, bias, act_ref):
    @pl.loop(0, count)
    def _(i):
        top = pl.multiple_of((i + first) * 32, 32)
        rows = pl.ds(top, 32)
        behind, ahead = bound_ref[0, rows, :], bound_ref[1, rows, :]
        for tile in range(CH // 128):
            lanes = slice(tile * 128, (tile + 1) * 128)
            depth = jnp.zeros((32, 128), F32)
            for j in range(KERNEL):
                source = glu_ref[tile, pl.ds(top + j + 1, 32), :]
                if j < HALF:
                    source = jnp.where(behind <= float(j - HALF), source, 0.0)
                elif j > HALF:
                    source = jnp.where(ahead > float(j - HALF), source, 0.0)
                depth = depth + taps[j : j + 1, lanes] * source
            moved = depth * gain[lanes].reshape(1, 128) + bias[lanes].reshape(1, 128)
            act_ref[rows, lanes] = (moved * jax.nn.sigmoid(moved)).astype(BF16)


def pool(copies, place, part_ref, give, take, sum_ref, sum16, rx, s2, rz, zb, xb, sb, out_ref):
    c = place.c
    copy = copies.send(give.at[1 - c], take, place.at(dc=1))
    copy.wait_recv()
    sum_ref[...] = part_ref[c] + take[...].astype(F32)
    sum16[...] = sum_ref[...].astype(BF16)
    got = []
    for k in range(1, NX):
        rows = pl.ds(pl.multiple_of((place.x + k) % NX * 32, 32), 32)
        got.append(copies.send(sum16.at[rows], rx.at[k - 1], place.at(dx=k)))
    total = sum_ref[pl.ds(pl.multiple_of(place.x * 32, 32), 32), :]
    for k, copy in enumerate(got):
        copy.wait_recv()
        total = total + rx[k].astype(F32)
    for j in range(NZ):
        s2[j] = total[8 * (j // 2) : 8 * (j // 2) + 8, 384 * (j % 2) : 384 * (j % 2) + 384]
    got = [copies.send(s2.at[(place.z + k) % NZ], rz.at[k - 1], place.at(dz=k)) for k in range(1, NZ)]
    total = s2[place.z]
    for k, copy in enumerate(got):
        copy.wait_recv()
        total = total + rz[k]
    zb[place.z] = total
    got = [copies.send(zb.at[place.z], zb.at[place.z], place.at(dz=k)) for k in range(1, NZ)]
    for copy in got:
        copy.wait_recv()
    parts = [jnp.concatenate([zb[2 * j], zb[2 * j + 1]], axis=1) for j in range(4)]
    xb[place.x] = jnp.concatenate(parts, axis=0).astype(BF16)
    got = [copies.send(xb.at[place.x], xb.at[place.x], place.at(dx=k)) for k in range(1, NX)]
    for copy in got:
        copy.wait_recv()
    copies.send(xb, sb, place.at(dc=1)).wait_recv()
    out_ref[c] = xb[...]
    out_ref[1 - c] = sb[...]


def block_kernel(
    h_frames, h_lengths, h_g_attn, h_wq, h_wk, h_wv, h_wo, h_g_conv, h_we, h_taps, h_bn_gain, h_bn_bias, h_ws, h_g_final,
    h_out, h_pooled,
    frames, lengths, g_attn, wq, wk, wv, wo, g_conv, we, taps, bn_gain, bn_bias, ws, g_final, out_ref, pooled_ref,
    g_ref, own_ref, w_kv, w_q, w_o, w_e, w_s, give, take, halo, normed, query, kv, ctx, after, glu16, glu_ref, rim, act,
    moved, bound_ref, member_ref, inverse_ref, part_ref, pool_give, pool_take, sum_ref, sum16, rx, s2, rz, zb, xb, sb,
    send_sem, recv_sem, load_sem,
):
    place = Place()
    barrier = pltpu.get_barrier_semaphore()
    partners = place.partners()
    for partner in partners:
        pl.semaphore_signal(barrier, inc=1, device_id=partner, device_id_type=MESH)
    pairs = (
        (h_wk, wk), (h_wv, wv), (h_wo, wo), (h_ws, ws), (h_frames, frames), (h_wq, wq), (h_we, we), (h_g_attn, g_attn),
        (h_lengths, lengths), (h_g_conv, g_conv), (h_taps, taps), (h_bn_gain, bn_gain), (h_bn_bias, bn_bias),
        (h_g_final, g_final),
    )
    loads = [pltpu.make_async_copy(src, dst, load_sem.at[k]) for k, (src, dst) in enumerate(pairs)]
    for load in loads:
        load.start()
    lead = place.c == 0
    for load in loads[:4]:
        load.wait()
    pack_own(own_ref, 0, wk[...].astype(F32), lead)
    pack_own(own_ref, 1, wv[...].astype(F32), lead)
    for k, ref in enumerate((wo, ws)):
        value = ref[...].astype(F32)
        theirs = jnp.where(lead, value[:, CH:], value[:, :CH])
        give[k] = jnp.concatenate([theirs, jnp.zeros((4, CH), F32)], axis=0).astype(BF16)
    for load in loads[4:]:
        load.wait()
    pl.semaphore_wait(barrier, len(partners))

    copies = Copies(send_sem, recv_sem)
    gather = Gather(copies, place, g_ref, own_ref)
    groups, sent = {}, {}

    def start(g):
        groups[g] = gather.start(g)
        if g == 0:
            sent["side"] = copies.send(give, take, place.at(dc=1))

    def pack_rest():
        pack_own(own_ref, 2, wq[...].astype(F32), lead)
        pack_own(own_ref, 4, we[:, :CH].astype(F32), lead)
        pack_own(own_ref, 5, we[:, CH:].astype(F32), lead)

    def pack_halves():
        sent["side"].wait_recv()
        for k, (unit, ref) in enumerate(((3, wo), (6, ws))):
            value = ref[...].astype(F32)
            own = jnp.where(lead, value[:, :CH], value[:, CH:])
            got = take[k].astype(F32)[:12]
            both = jnp.where(lead, jnp.concatenate([own, got], axis=0), jnp.concatenate([got, own], axis=0))
            pack_own(own_ref, unit, both, place.x % 2 == 0)

    def arrived(unit):
        for g, (first, end, _, _) in enumerate(GROUPS):
            if first <= unit < end:
                assert groups[g].finish()

    def lay_kv():
        arrived(0)
        lay_rows(g_ref, 0, w_kv, 0)
        lay_rows(g_ref, 1, w_kv, CH)

    far = pl.ds(pl.multiple_of(place.c * (2 * ROWS), ROWS), ROWS)

    def send_frames():
        sent["frames"] = copies.send(frames, halo, place.beside(2 * place.c - 1))

    def norm_halo(first, end):
        if first == 0:
            sent["frames"].wait_recv()
        norm_into(halo, g_attn, normed.at[pl.ds(ROWS, ROWS)], first, end)

    def make_kv(half):
        @pl.loop(half * 3, half * 3 + 3)
        def _(n):
            cols = pl.ds(pl.multiple_of(n * 256, 256), 256)
            both = times(normed, w_kv, n * 256).astype(BF16)
            kv[ROWS : 2 * ROWS, cols] = both[:ROWS]
            kv[far, cols] = both[ROWS:]

    def send_kv():
        sent["kv"] = copies.send(kv.at[pl.ds(ROWS, ROWS)], kv.at[far], place.at(dc=1))

    def lay_q():
        arrived(2)
        lay_rows(g_ref, 2, w_q, 0)

    def make_q():
        @pl.loop(0, 3)
        def _(n):
            query[:, pl.ds(pl.multiple_of(n * 256, 256), 256)] = times(normed.at[pl.ds(0, ROWS)], w_q, n * 256).astype(BF16)

    def lay_o():
        arrived(3)
        lay_halves(g_ref, 3, w_o)

    def attention(k):
        if k == 0:
            sent["kv"].wait_recv()
        attend(k, query, kv, bound_ref, ctx)

    def make_after():
        @pl.loop(0, 6)
        def _(n):
            cols = pl.ds(pl.multiple_of(n * 256, 256), 256)
            after[:, cols] = (frames[:, cols].astype(F32) + times(ctx, w_o, n * 256)).astype(BF16)

    def lay_e():
        arrived(4)
        lay_rows(g_ref, 4, w_e, 0)
        lay_rows(g_ref, 5, w_e, CH)

    def make_glu(n):
        gate = times(normed.at[pl.ds(0, ROWS)], w_e, CH + n * 256)
        value = times(normed.at[pl.ds(0, ROWS)], w_e, n * 256)
        glu = (value * jax.nn.sigmoid(gate)).astype(BF16)
        glu16[:, n * 256 : n * 256 + 256] = glu
        wide = glu.astype(F32)
        glu_ref[2 * n, 16 : 16 + ROWS, :] = wide[:, :128]
        glu_ref[2 * n + 1, 16 : 16 + ROWS, :] = wide[:, 128:]

    def send_rim():
        sent["rim0"] = copies.send(glu16.at[pl.ds(0, 16)], rim.at[1], place.beside(-1))
        sent["rim1"] = copies.send(glu16.at[pl.ds(ROWS - 16, 16)], rim.at[0], place.beside(1))

    def conv(first, count):
        convolve(first, count, glu_ref, bound_ref, taps, bn_gain, bn_bias, act)

    def conv_edges():
        sent["rim0"].wait_recv()
        sent["rim1"].wait_recv()
        for tile in range(CH // 128):
            lanes = slice(tile * 128, (tile + 1) * 128)
            glu_ref[tile, :16, :] = rim[0, :, lanes].astype(F32)
            glu_ref[tile, 16 + ROWS :, :] = rim[1, :, lanes].astype(F32)
        conv(0, 1)
        conv(7, 1)

    def lay_s():
        arrived(6)
        lay_halves(g_ref, 6, w_s)

    def make_moved():
        @pl.loop(0, 6)
        def _(n):
            cols = pl.ds(pl.multiple_of(n * 256, 256), 256)
            moved[:, cols] = after[:, cols].astype(F32) + times(act, w_s, n * 256)

    def finish():
        norm_into(moved, g_final, out_ref, 0, 8)
        sent["out"] = pltpu.make_async_copy(out_ref, h_out, load_sem.at[len(pairs)])
        sent["out"].start()
        for h in range(2):
            for n in range(3):
                cols = slice(h * CH + n * 256, h * CH + n * 256 + 256)
                sums = jnp.dot(member_ref[...], out_ref[:, cols], preferred_element_type=F32) * inverse_ref[:, :1]
                part_ref[h, :, n * 256 : n * 256 + 256] = sums
                pool_give[h, :, n * 256 : n * 256 + 256] = sums.astype(BF16)

    tasks = {
        "packrest": pack_rest,
        "packos": pack_halves,
        "bounds": lambda: bounds(lengths, place, bound_ref, member_ref, inverse_ref),
        "norma": lambda: norm_into(frames, g_attn, normed, 0, 4),
        "normb": lambda: norm_into(frames, g_attn, normed, 4, 8),
        "sendfr": send_frames,
        "normx": lambda: norm_halo(0, 4),
        "normy": lambda: norm_halo(4, 8),
        "laykv": lay_kv,
        "mmkv0": lambda: make_kv(0),
        "mmkv1": lambda: make_kv(1),
        "sendkv": send_kv,
        "layq": lay_q,
        "mmq": make_q,
        "layo": lay_o,
        "att0": lambda: attention(0),
        "att1": lambda: attention(1),
        "att2": lambda: attention(2),
        "att3": lambda: attention(3),
        "mmo": make_after,
        "normc": lambda: norm_into(after, g_conv, normed, 0, 4),
        "normd": lambda: norm_into(after, g_conv, normed, 4, 8),
        "laye": lay_e,
        "mme0": lambda: make_glu(0),
        "mme1": lambda: make_glu(1),
        "mme2": lambda: make_glu(2),
        "sendrim": send_rim,
        "conv0": lambda: conv(1, 3),
        "conv1": lambda: conv(4, 3),
        "lays": lay_s,
        "conv2": conv_edges,
        "mms": make_moved,
        "fin": finish,
    }
    for name in PLAN:
        if name.startswith("start"):
            start(int(name[5:]))
        elif name[0].isdigit():
            groups[int(name[0])].step(int(name[1]))
        else:
            tasks[name]()
    pool(copies, place, part_ref, pool_give, pool_take, sum_ref, sum16, rx, s2, rz, zb, xb, sb, pooled_ref)
    last = pltpu.make_async_copy(pooled_ref, h_pooled, load_sem.at[len(pairs) + 1])
    last.start()
    copies.finish()
    sent["out"].wait()
    last.wait()


def local(frames, lengths, norm_attn, w_query, w_key, w_value, w_out, norm_conv, w_expand, kernel, bn_gain,
          bn_bias, w_shrink, norm_final):
    hbm = pl.BlockSpec(memory_space=pl.ANY)
    block_out, halves = pl.pallas_call(
        block_kernel,
        out_shape=[
            jax.ShapeDtypeStruct((ROWS, D), BF16),
            jax.ShapeDtypeStruct((2, NX, 32, CH), BF16),
        ],
        in_specs=[hbm] * 14,
        out_specs=[hbm] * 2,
        scratch_shapes=[
            pltpu.VMEM((ROWS, D), BF16),
            pltpu.VMEM((1, NREC), jnp.int32),
            pltpu.VMEM((D,), F32),
            pltpu.VMEM((24, CH), BF16),
            pltpu.VMEM((24, CH), BF16),
            pltpu.VMEM((24, CH), BF16),
            pltpu.VMEM((12, D), BF16),
            pltpu.VMEM((D,), F32),
            pltpu.VMEM((24, D), BF16),
            pltpu.VMEM((KERNEL, CH), F32),
            pltpu.VMEM((CH,), F32),
            pltpu.VMEM((CH,), F32),
            pltpu.VMEM((12, D), BF16),
            pltpu.VMEM((D,), F32),
            pltpu.VMEM((ROWS, D), BF16),
            pltpu.VMEM((2, NX, 32, CH), BF16),
            pltpu.VMEM((NZ, NX, 2, 16, COLS), BF16),
            pltpu.VMEM((16, COLS), BF16),
            pltpu.VMEM((D, 2 * CH), BF16),
            pltpu.VMEM((D, CH), BF16),
            pltpu.VMEM((CH, D), BF16),
            pltpu.VMEM((D, 2 * CH), BF16),
            pltpu.VMEM((CH, D), BF16),
            pltpu.VMEM((2, 16, CH), BF16),
            pltpu.VMEM((2, 16, CH), BF16),
            pltpu.VMEM((ROWS, D), BF16),
            pltpu.VMEM((2 * ROWS, D), BF16),
            pltpu.VMEM((ROWS, CH), BF16),
            pltpu.VMEM((3 * ROWS, 2 * CH), BF16),
            pltpu.VMEM((ROWS, CH), BF16),
            pltpu.VMEM((ROWS, D), BF16),
            pltpu.VMEM((ROWS, CH), BF16),
            pltpu.VMEM((CH // 128, ROWS + 32, 128), F32),
            pltpu.VMEM((2, 16, CH), BF16),
            pltpu.VMEM((ROWS, CH), BF16),
            pltpu.VMEM((ROWS, D), F32),
            pltpu.VMEM((2, ROWS, NREC), F32),
            pltpu.VMEM((NREC, ROWS), BF16),
            pltpu.VMEM((NREC, NREC), F32),
            pltpu.VMEM((2, NREC, CH), F32),
            pltpu.VMEM((2, NREC, CH), BF16),
            pltpu.VMEM((NREC, CH), BF16),
            pltpu.VMEM((NREC, CH), F32),
            pltpu.VMEM((NREC, CH), BF16),
            pltpu.VMEM((NX - 1, 32, CH), BF16),
            pltpu.VMEM((NZ, 8, 384), F32),
            pltpu.VMEM((NZ - 1, 8, 384), F32),
            pltpu.VMEM((NZ, 8, 384), F32),
            pltpu.VMEM((NX, 32, CH), BF16),
            pltpu.VMEM((NX, 32, CH), BF16),
            pltpu.SemaphoreType.DMA((N_COPIES,)),
            pltpu.SemaphoreType.DMA((N_COPIES,)),
            pltpu.SemaphoreType.DMA((16,)),
        ],
        compiler_params=pltpu.CompilerParams(
            collective_id=0, has_side_effects=True, vmem_limit_bytes=60 << 20
        ),
        cost_estimate=pl.CostEstimate(flops=5_000_000_000, bytes_accessed=20_000_000, transcendentals=3_000_000),
    )(
        frames, lengths.reshape(1, NREC), norm_attn, w_query, w_key, w_value, w_out,
        norm_conv, w_expand, kernel, bn_gain, bn_bias, w_shrink,
        norm_final,
    )
    halves = halves.reshape(2, NREC, CH).astype(F32)
    return block_out, jnp.concatenate([halves[0], halves[1]], axis=1)


def solution(mesh):
    return jax.shard_map(
        local,
        mesh=mesh,
        in_specs=(
            P(("rep", "seq"), None),
            P("rep"),
            P(),
            P("seq", None),
            P("seq", None),
            P("seq", None),
            P("seq", None),
            P(),
            P("seq", None),
            P(),
            P(),
            P(),
            P("seq", None),
            P(),
        ),
        out_specs=(P(("rep", "seq"), None), P("rep", None)),
        check_vma=False,
    )
```

```python
import jax
import jax.numpy as jnp
from jax import lax
from jax.experimental import pallas as pl
from jax.experimental.pallas import tpu as pltpu
from jax.sharding import PartitionSpec as P

H = 8
HD = 96
KERNEL = 31
HALF = 15
MESH = pl.DeviceIdType.MESH
F32 = jnp.float32
BF16 = jnp.bfloat16
NZ, NX, NY = 8, 4, 4
ROWS = 256
D = 1536
CH = 768
NREC = 128
UNIT = 1152
COLS = 7 * UNIT
GROUPS = (
    (0, 2, (7, 7, 4), ('straight', 'ring', 'ring', 'ring', 'straight')),
    (2, 4, (7, 3, 8), ('straight', 'ring', 'ring', 'ring', 'hops')),
    (4, 6, (5, 5, 8), ('ring', 'ring', 'ring', 'ring', 'straight')),
    (6, 7, (1, 0, 8), ('straight', 'ring', 'hops', 'ring', 'ring')),
)
N_COPIES = 71
PLAN = (
    "start0", "sendfr", "packrest", "bounds", "packos", "01", "start1", "00", "02", "start3", "norma",
    "normb", "01", "11", "12", "start2", "00", "32", "01", "11", "12", "21", "normx", "normy", "10", "22",
    "02", "30", "20", "00", "32", "01", "11", "21", "12", "22", "10", "20", "30", "02", "00", "32", "11",
    "21", "10", "12", "20", "02", "30", "01", "00", "32", "22", "21", "laykv", "12", "10", "mmkv0", "11",
    "20", "mmkv1", "10", "32", "sendkv", "layq", "mmq", "22", "20", "layo", "21", "att0", "att1", "att2",
    "20", "att3", "21", "32", "mmo", "normc", "22", "normd", "laye", "mme0", "mme1", "32", "mme2", "sendrim",
    "conv0", "conv1", "lays", "conv2", "mms", "fin",
)


class Place:
    def __init__(self):
        self.index = lax.axis_index("seq")
        self.z = self.index // 8
        self.x = (self.index // 2) % 4
        self.c = self.index % 2
        self.y = lax.axis_index("rep")

    def at(self, dz=0, dx=0, dc=0, dy=0):
        z = (self.z + dz + NZ) % NZ
        x = (self.x + dx + NX) % NX
        c = (self.c + dc) % 2
        y = (self.y + dy + NY) % NY
        return {"seq": z * 8 + x * 2 + c, "rep": y}

    def beside(self, step):
        return {"seq": (self.index + step + 64) % 64, "rep": self.y}

    def partners(self):
        found = [self.at(dz=k) for k in range(1, NZ)]
        found += [self.at(dx=k) for k in range(1, NX)]
        found += [self.at(dy=k) for k in range(1, NY)]
        found += [self.at(dc=1), self.beside(2 * self.c - 1)]
        return found


class Copies:
    def __init__(self, send_sem, recv_sem):
        self.send_sem, self.recv_sem = send_sem, recv_sem
        self.count = 0
        self.all = []

    def sems(self):
        self.count += 1
        return {"send_sem": self.send_sem.at[self.count - 1], "recv_sem": self.recv_sem.at[self.count - 1]}

    def send(self, src, dst, device):
        copy = pltpu.make_async_remote_copy(
            src_ref=src, dst_ref=dst, device_id=device, device_id_type=MESH, **self.sems()
        )
        copy.start()
        self.all.append(copy)
        return copy

    def finish(self):
        for copy in self.all:
            copy.wait_send()


class Batch:
    def __init__(self, copies, ref, whole, device):
        self.ref, self.sems = ref, copies.sems()
        self.total = self.make(whole, device)
        copies.all.append(self)

    def make(self, region, device):
        part = self.ref.at[region]
        return pltpu.make_async_remote_copy(
            src_ref=part, dst_ref=part, device_id=device, device_id_type=MESH, **self.sems
        )

    def push(self, region, device):
        self.make(region, device).start()

    def wait_recv(self):
        self.total.wait_recv()

    def wait_send(self):
        self.total.wait_send()


class Gather:
    def __init__(self, copies, place, ref, own):
        self.copies, self.place, self.ref, self.own = copies, place, ref, own

    def batch(self, whole):
        return Batch(self.copies, self.ref, whole, self.place.at(dc=1))

    def straight(self, axis, n, region, many, shared):
        place = self.place
        me = {"z": place.z, "x": place.x, "y": place.y}[axis]
        sent = self.batch(many(n - 1))
        for k in range(1, n):
            sent.push(region(me, None), place.at(**{"d" + axis: k}))
        yield
        sent.wait_recv()
        for k in range(1, n):
            shared.push(region((me - k + n) % n, None), place.at(dc=1))

    def hops(self, region, many, shared):
        place = self.place
        me, other = place.z, place.at(dc=1)
        block = lambda k: region((me + k + NZ) % NZ, None)
        sent = self.batch(many(4))
        for k in (1, -1, 2, -2):
            sent.push(block(0), place.at(dz=k))
        yield
        sent.wait_recv()
        sent = self.batch(many(3))
        for k in (1, -1):
            sent.push(block(-2 * k), place.at(dz=k))
        for k in (1, -1):
            half = region((me - 2 * k + NZ) % NZ, 0 if k == 1 else 1)
            if half is not None:
                sent.push(half, place.at(dz=2 * k))
        for k in (1, -1, 2, -2):
            shared.push(block(k), other)
        yield
        sent.wait_recv()
        for k in (3, -3, 4):
            shared.push(block(k), other)

    def ring(self, axis, region, many, shared):
        place = self.place
        n = {"z": NZ, "x": NX, "y": NY}[axis]
        me = {"z": place.z, "x": place.x, "y": place.y}[axis]
        up, down, other = place.at(**{"d" + axis: 1}), place.at(**{"d" + axis: -1}), place.at(dc=1)
        sent = self.batch(many(2))
        sent.push(region(me, None), up)
        sent.push(region(me, None), down)
        for step in range(1, n // 2):
            low, high = (me - step + n) % n, (me + step) % n
            last = step == n // 2 - 1
            yield
            sent.wait_recv()
            sent = self.batch(many(1 if last else 2))
            sent.push(region(low, 0 if last else None), up)
            rest = region(high, 1 if last else None)
            if rest is not None:
                sent.push(rest, down)
            shared.push(region(low, None), other)
            shared.push(region(high, None), other)
        yield
        sent.wait_recv()
        shared.push(region((me + n // 2) % n, None), other)

    def part(self, order, lo, tiles, modes, shared):
        place = self.place
        quarter = tiles // 4 if "y" in order else tiles

        def cut(k, half, count):
            start, size = 0, count * 128
            if half is not None:
                first = (count + 1) // 2 * 128
                start, size = (0, first) if half == 0 else (first, size - first)
            if "y" not in order:
                return pl.ds(lo + start, size)
            return pl.ds(pl.multiple_of(lo + k * (quarter * 128) + start, 128), size)

        done = set()
        for axis in order:

            def region(k, half, axis=axis, done=frozenset(done)):
                at = {"z": place.z, "x": place.x, "y": place.y}
                at[axis] = k
                z = slice(None) if "z" in done else at["z"]
                x = slice(None) if "x" in done else at["x"]
                if half == 1 and quarter == 1:
                    return None
                return (z, x, place.c, slice(None), cut(at["y"], half, quarter))

            def many(count, axis=axis, region=region):
                at = list(region({"z": place.z, "x": place.x, "y": place.y}[axis], None))
                if axis == "y":
                    at[4] = pl.ds(lo, count * quarter * 128)
                else:
                    at["zx".index(axis)] = pl.ds(0, count)
                return tuple(at)

            mode = modes[axis]
            if mode == "hops":
                yield from self.hops(region, many, shared)
            elif mode == "ring":
                yield from self.ring(axis, region, many, shared)
            else:
                yield from self.straight(axis, {"z": NZ, "x": NX, "y": NY}[axis], region, many, shared)
            done.add(axis)

    def start(self, group):
        place = self.place
        first, end, tiles, ways = GROUPS[group]
        lo, hi = first * UNIT, end * UNIT
        quarter = tiles[2] * 32
        mid = hi - 4 * quarter
        shared = self.batch((slice(None), slice(None), place.c, slice(None), pl.ds(lo, hi - lo)))
        spans = []
        if mid > lo:
            spans.append(pl.ds(lo, mid - lo))
        if quarter:
            spans.append(pl.ds(pl.multiple_of(mid + place.y * quarter, 128), quarter))
        for cols in spans:
            region = (place.z, place.x, place.c, slice(None), cols)
            self.ref[region] = self.own[:, cols]
            shared.push(region, place.at(dc=1))
        parts = {}
        for k, (order, count) in enumerate(zip(("xz", "zx", "zxy"), tiles)):
            if count:
                parts[k] = self.part(order, lo, count, {"x": ways[0], "y": ways[1], "z": ways[2 + k]}, shared)
                lo += count * 128
        return Group(parts, shared)


class Group:
    def __init__(self, parts, shared):
        self.parts, self.shared = parts, shared
        for part in parts.values():
            next(part)

    def step(self, k):
        if next(self.parts[k], True) is not None:
            del self.parts[k]

    def finish(self):
        if self.shared is not None:
            self.shared.wait_recv()
        self.shared = None
        return not self.parts


def fold(rows8):
    half = rows8.shape[1] // 2
    return jnp.concatenate([rows8[:, :half], rows8[:, half:]], axis=0)


def pack_own(own_ref, unit, value, first):
    main = jnp.where(first, value[:16], value[8:])
    rest = jnp.where(first, value[16:], value[:8])
    whole = jnp.concatenate([main, fold(rest)], axis=1).astype(BF16)
    own_ref[:, unit * UNIT : (unit + 1) * UNIT] = whole


def unfold(low, high):
    low, high = low.astype(F32), high.astype(F32)
    left = jnp.concatenate([low[:8], high[:8]], axis=0)
    right = jnp.concatenate([low[8:], high[8:]], axis=0)
    return jnp.concatenate([left, right], axis=1).astype(BF16)


def lay_rows(g_ref, unit, w_ref, column):
    lo = unit * UNIT

    @pl.loop(0, NZ)
    def _(z):
        for x in range(NX):
            row = z * 192 + x * 48
            low, high = g_ref[z, x, 0, :, lo : lo + UNIT], g_ref[z, x, 1, :, lo : lo + UNIT]
            for k, value in enumerate((low[:, :CH], unfold(low[:, CH:], high[:, CH:]), high[:, :CH])):
                w_ref[pl.ds(pl.multiple_of(row + 16 * k, 16), 16), column : column + CH] = value


def lay_halves(g_ref, unit, w_ref):
    lo = unit * UNIT

    @pl.loop(0, NZ)
    def _(z):
        for pair in range(2):
            for c in range(2):
                row = z * 96 + pair * 48
                low = g_ref[z, 2 * pair, c, :, lo : lo + UNIT]
                high = g_ref[z, 2 * pair + 1, c, :, lo : lo + UNIT]
                for k, value in enumerate((low[:, :CH], unfold(low[:, CH:], high[:, CH:]), high[:, :CH])):
                    w_ref[pl.ds(pl.multiple_of(row + 16 * k, 16), 16), c * CH : (c + 1) * CH] = value


def norm_rows(values, gain):
    mean = jnp.mean(values, axis=-1, keepdims=True)
    centred = values - mean
    var = jnp.mean(centred * centred, axis=-1, keepdims=True)
    return centred * lax.rsqrt(var + 1e-05) * gain


def norm_into(src, gain, dst, first, end):
    @pl.loop(first, end)
    def _(i):
        rows = pl.ds(pl.multiple_of(i * 32, 32), 32)
        dst[rows, :] = norm_rows(src[rows, :].astype(F32), gain[...].reshape(1, D)).astype(BF16)


def times(x_ref, w_ref, column):
    return jnp.dot(
        x_ref[...], w_ref[:, pl.ds(pl.multiple_of(column, 256), 256)], preferred_element_type=F32
    )


def bounds(len_ref, place, bound_ref, member_ref, inverse_ref):
    lengths = len_ref[...].astype(F32)
    row = lax.broadcasted_iota(jnp.int32, (NREC, NREC), 0)
    col = lax.broadcasted_iota(jnp.int32, (NREC, NREC), 1)
    before = (row <= col).astype(BF16)
    wide = jnp.broadcast_to(lengths, (NREC, NREC))
    ends = jnp.dot(wide.astype(BF16), before, preferred_element_type=F32)
    first = (place.index * ROWS).astype(F32)
    t = lax.broadcasted_iota(jnp.int32, (ROWS, NREC), 0).astype(F32) + first
    end_row = jnp.broadcast_to(ends[:1], (ROWS, NREC))
    begin = jnp.max(jnp.where(end_row <= t, end_row, 0.0), axis=1, keepdims=True)
    finish = jnp.min(jnp.where(end_row > t, end_row, 65536.0), axis=1, keepdims=True)
    bound_ref[0] = jnp.broadcast_to(begin, (ROWS, NREC)) - t
    bound_ref[1] = jnp.broadcast_to(finish, (ROWS, NREC)) - t
    eye = row == col
    end_col = jnp.sum(jnp.where(eye, ends, 0.0), axis=1, keepdims=True)
    len_col = jnp.sum(jnp.where(eye, wide, 0.0), axis=1, keepdims=True)
    inverse_ref[...] = jnp.broadcast_to(1.0 / len_col, (NREC, NREC))
    at = lax.broadcasted_iota(jnp.int32, (NREC, ROWS), 1).astype(F32) + first
    inside = (at < end_col) & (at >= end_col - len_col)
    member_ref[...] = inside.astype(F32).astype(BF16)


def attend(i, q_ref, kv_ref, bound_ref, ctx_ref):
    factor = 1.4426950408889634 / HD**0.5
    span = 640

    top, lane0 = (i // 2) * 128, (i % 2) * 384
    rows = pl.ds(pl.multiple_of(top, 128), 128)
    window = pl.ds(pl.multiple_of(top, 128), span)
    offset = lax.broadcasted_iota(jnp.int32, (128, span), 1) - lax.broadcasted_iota(jnp.int32, (128, span), 0)
    offset = (offset - ROWS).astype(F32)
    inside = (offset >= bound_ref[0, rows, :1]) & (offset < bound_ref[1, rows, :1])
    bias = jnp.where(inside, 0.0, -1e30)
    outs = []
    for h in range(4):
        lo, hi = h * HD, (h + 1) * HD
        a, b = lo // 128 * 128, (hi + 127) // 128 * 128
        lane = lax.broadcasted_iota(jnp.int32, (128, b - a), 1) + a
        cols = pl.ds(pl.multiple_of(lane0 + a, 128), b - a)
        q = q_ref[rows, cols]
        q = jnp.where((lane >= lo) & (lane < hi), q.astype(F32), 0.0).astype(BF16)
        score = lax.dot_general(
            q, kv_ref[window, cols], (((1,), (1,)), ((), ())), preferred_element_type=F32
        )
        score = score + bias
        peak = jnp.max(score, axis=1, keepdims=True)
        expo = jnp.exp2((score - peak) * factor)
        total = jnp.sum(expo, axis=1, keepdims=True)
        values = kv_ref[window, pl.ds(pl.multiple_of(CH + lane0 + a, 128), b - a)]
        out = jnp.dot(expo.astype(BF16), values, preferred_element_type=F32)
        outs.append((a, out / total))
    for tile in range(3):
        lane = lax.broadcasted_iota(jnp.int32, (128, 128), 1)
        at = tile * 128
        one, two = outs[tile], outs[tile + 1]
        left = one[1][:, at - one[0] : at - one[0] + 128]
        right = two[1][:, at - two[0] : at - two[0] + 128]
        whole = jnp.where(lane < (tile + 1) * HD - at, left, right).astype(BF16)
        ctx_ref[rows, pl.ds(pl.multiple_of(lane0 + at, 128), 128)] = whole


def convolve(first, count, glu_ref, bound_ref, taps, gain, bias, act_ref):
    @pl.loop(0, count)
    def _(i):
        top = pl.multiple_of((i + first) * 32, 32)
        rows = pl.ds(top, 32)
        behind, ahead = bound_ref[0, rows, :], bound_ref[1, rows, :]
        for tile in range(CH // 128):
            lanes = slice(tile * 128, (tile + 1) * 128)
            depth = jnp.zeros((32, 128), F32)
            for j in range(KERNEL):
                source = glu_ref[tile, pl.ds(top + j + 1, 32), :]
                if j < HALF:
                    source = jnp.where(behind <= float(j - HALF), source, 0.0)
                elif j > HALF:
                    source = jnp.where(ahead > float(j - HALF), source, 0.0)
                depth = depth + taps[j : j + 1, lanes] * source
            moved = depth * gain[lanes].reshape(1, 128) + bias[lanes].reshape(1, 128)
            act_ref[rows, lanes] = (moved * jax.nn.sigmoid(moved)).astype(BF16)


def pool(copies, place, part_ref, give, take, sum_ref, sum16, rx, s2, rz, zb, xb, sb, out_ref):
    c = place.c
    copy = copies.send(give.at[1 - c], take, place.at(dc=1))
    copy.wait_recv()
    sum_ref[...] = part_ref[c] + take[...].astype(F32)
    sum16[...] = sum_ref[...].astype(BF16)
    def exchange(axis, n, src, dst, size):
        sems = copies.sems()

        def make(src, dst, device):
            return pltpu.make_async_remote_copy(
                src_ref=src, dst_ref=dst, device_id=device, device_id_type=MESH, **sems
            )

        for k in range(1, n):
            make(src(k), dst(k), place.at(**{"d" + axis: k})).start()
        total = make(size, size, place.at(dc=1))
        copies.all.append(total)
        total.wait_recv()

    def mine(k):
        return sum16.at[pl.ds(pl.multiple_of((place.x + k) % NX * 32, 32), 32)]

    exchange("x", NX, mine, lambda k: rx.at[k - 1], rx)
    total = sum_ref[pl.ds(pl.multiple_of(place.x * 32, 32), 32), :]
    for k in range(NX - 1):
        total = total + rx[k].astype(F32)
    for j in range(NZ):
        s2[j] = total[8 * (j // 2) : 8 * (j // 2) + 8, 384 * (j % 2) : 384 * (j % 2) + 384]
    exchange("z", NZ, lambda k: s2.at[(place.z + k) % NZ], lambda k: rz.at[k - 1], rz)
    total = s2[place.z]
    for k in range(NZ - 1):
        total = total + rz[k]
    zb[place.z] = total
    exchange("z", NZ, lambda k: zb.at[place.z], lambda k: zb.at[place.z], rz)
    parts = [jnp.concatenate([zb[2 * j], zb[2 * j + 1]], axis=1) for j in range(4)]
    xb[place.x] = jnp.concatenate(parts, axis=0).astype(BF16)
    exchange("x", NX, lambda k: xb.at[place.x], lambda k: xb.at[place.x], rx)
    copies.send(xb, sb, place.at(dc=1)).wait_recv()
    for k in range(NX):
        rows = slice(32 * k, 32 * k + 32)
        out_ref[rows, pl.ds(pl.multiple_of(c * CH, CH), CH)] = xb[k]
        out_ref[rows, pl.ds(pl.multiple_of((1 - c) * CH, CH), CH)] = sb[k]


def block_kernel(
    h_frames, h_lengths, h_g_attn, h_wq, h_wk, h_wv, h_wo, h_g_conv, h_we, h_taps, h_bn_gain, h_bn_bias, h_ws, h_g_final,
    h_out, h_pooled,
    frames, lengths, g_attn, wq, wk, wv, wo, g_conv, we, taps, bn_gain, bn_bias, ws, g_final, out_ref, pooled_ref,
    g_ref, own_ref, w_kv, w_q, w_o, w_e, w_s, give, take, halo, normed, query, kv, ctx, after, glu16, glu_ref, rim, act,
    moved, bound_ref, member_ref, inverse_ref, part_ref, pool_give, pool_take, sum_ref, sum16, rx, s2, rz, zb, xb, sb,
    send_sem, recv_sem, load_sem,
):
    place = Place()
    barrier = pltpu.get_barrier_semaphore()
    partners = place.partners()
    for partner in partners:
        pl.semaphore_signal(barrier, inc=1, device_id=partner, device_id_type=MESH)
    pairs = (
        (h_wk, wk), (h_wv, wv), (h_wo, wo), (h_ws, ws), (h_frames, frames), (h_wq, wq), (h_we, we), (h_g_attn, g_attn),
        (h_lengths, lengths), (h_g_conv, g_conv), (h_taps, taps), (h_bn_gain, bn_gain), (h_bn_bias, bn_bias),
        (h_g_final, g_final),
    )
    loads = [pltpu.make_async_copy(src, dst, load_sem.at[k]) for k, (src, dst) in enumerate(pairs)]
    for load in loads:
        load.start()
    lead = place.c == 0
    for load in loads[:4]:
        load.wait()
    pack_own(own_ref, 0, wk[...].astype(F32), lead)
    pack_own(own_ref, 1, wv[...].astype(F32), lead)
    for k, ref in enumerate((wo, ws)):
        value = ref[...].astype(F32)
        theirs = jnp.where(lead, value[:, CH:], value[:, :CH])
        give[k] = jnp.concatenate([theirs, jnp.zeros((4, CH), F32)], axis=0).astype(BF16)
    for load in loads[4:]:
        load.wait()
    pl.semaphore_wait(barrier, len(partners))

    copies = Copies(send_sem, recv_sem)
    gather = Gather(copies, place, g_ref, own_ref)
    groups, sent = {}, {}

    def start(g):
        groups[g] = gather.start(g)
        if g == 0:
            sent["side"] = copies.send(give, take, place.at(dc=1))

    def pack_rest():
        pack_own(own_ref, 2, wq[...].astype(F32), lead)
        pack_own(own_ref, 4, we[:, :CH].astype(F32), lead)
        pack_own(own_ref, 5, we[:, CH:].astype(F32), lead)

    def pack_halves():
        sent["side"].wait_recv()
        for k, (unit, ref) in enumerate(((3, wo), (6, ws))):
            value = ref[...].astype(F32)
            own = jnp.where(lead, value[:, :CH], value[:, CH:])
            got = take[k].astype(F32)[:12]
            both = jnp.where(lead, jnp.concatenate([own, got], axis=0), jnp.concatenate([got, own], axis=0))
            pack_own(own_ref, unit, both, place.x % 2 == 0)

    def arrived(unit):
        for g, (first, end, _, _) in enumerate(GROUPS):
            if first <= unit < end:
                assert groups[g].finish()

    def lay_kv():
        arrived(0)
        lay_rows(g_ref, 0, w_kv, 0)
        lay_rows(g_ref, 1, w_kv, CH)

    far = pl.ds(pl.multiple_of(place.c * (2 * ROWS), ROWS), ROWS)

    def send_frames():
        sent["frames"] = copies.send(frames, halo, place.beside(2 * place.c - 1))

    def norm_halo(first, end):
        if first == 0:
            sent["frames"].wait_recv()
        norm_into(halo, g_attn, normed.at[pl.ds(ROWS, ROWS)], first, end)

    def make_kv(half):
        @pl.loop(half * 3, half * 3 + 3)
        def _(n):
            cols = pl.ds(pl.multiple_of(n * 256, 256), 256)
            both = times(normed, w_kv, n * 256).astype(BF16)
            kv[ROWS : 2 * ROWS, cols] = both[:ROWS]
            kv[far, cols] = both[ROWS:]

    def send_kv():
        sent["kv"] = copies.send(kv.at[pl.ds(ROWS, ROWS)], kv.at[far], place.at(dc=1))

    def lay_q():
        arrived(2)
        lay_rows(g_ref, 2, w_q, 0)

    def make_q():
        @pl.loop(0, 3)
        def _(n):
            query[:, pl.ds(pl.multiple_of(n * 256, 256), 256)] = times(normed.at[pl.ds(0, ROWS)], w_q, n * 256).astype(BF16)

    def lay_o():
        arrived(3)
        lay_halves(g_ref, 3, w_o)

    def attention(k):
        if k == 0:
            sent["kv"].wait_recv()
        attend(k, query, kv, bound_ref, ctx)

    def make_after():
        @pl.loop(0, 6)
        def _(n):
            cols = pl.ds(pl.multiple_of(n * 256, 256), 256)
            after[:, cols] = (frames[:, cols].astype(F32) + times(ctx, w_o, n * 256)).astype(BF16)

    def lay_e():
        arrived(4)
        lay_rows(g_ref, 4, w_e, 0)
        lay_rows(g_ref, 5, w_e, CH)

    def make_glu(n):
        gate = times(normed.at[pl.ds(0, ROWS)], w_e, CH + n * 256)
        value = times(normed.at[pl.ds(0, ROWS)], w_e, n * 256)
        glu = (value * jax.nn.sigmoid(gate)).astype(BF16)
        glu16[:, n * 256 : n * 256 + 256] = glu
        wide = glu.astype(F32)
        glu_ref[2 * n, 16 : 16 + ROWS, :] = wide[:, :128]
        glu_ref[2 * n + 1, 16 : 16 + ROWS, :] = wide[:, 128:]

    def send_rim():
        sent["rim0"] = copies.send(glu16.at[pl.ds(0, 16)], rim.at[1], place.beside(-1))
        sent["rim1"] = copies.send(glu16.at[pl.ds(ROWS - 16, 16)], rim.at[0], place.beside(1))

    def conv(first, count):
        convolve(first, count, glu_ref, bound_ref, taps, bn_gain, bn_bias, act)

    def conv_edges():
        sent["rim0"].wait_recv()
        sent["rim1"].wait_recv()
        for tile in range(CH // 128):
            lanes = slice(tile * 128, (tile + 1) * 128)
            glu_ref[tile, :16, :] = rim[0, :, lanes].astype(F32)
            glu_ref[tile, 16 + ROWS :, :] = rim[1, :, lanes].astype(F32)
        conv(0, 1)
        conv(7, 1)

    def lay_s():
        arrived(6)
        lay_halves(g_ref, 6, w_s)

    def make_moved():
        @pl.loop(0, 6)
        def _(n):
            cols = pl.ds(pl.multiple_of(n * 256, 256), 256)
            moved[:, cols] = after[:, cols].astype(F32) + times(act, w_s, n * 256)

    def finish():
        norm_into(moved, g_final, out_ref, 0, 8)
        sent["out"] = pltpu.make_async_copy(out_ref, h_out, load_sem.at[len(pairs)])
        sent["out"].start()
        for h in range(2):
            for n in range(3):
                cols = slice(h * CH + n * 256, h * CH + n * 256 + 256)
                sums = jnp.dot(member_ref[...], out_ref[:, cols], preferred_element_type=F32) * inverse_ref[:, :1]
                part_ref[h, :, n * 256 : n * 256 + 256] = sums
                pool_give[h, :, n * 256 : n * 256 + 256] = sums.astype(BF16)

    tasks = {
        "packrest": pack_rest,
        "packos": pack_halves,
        "bounds": lambda: bounds(lengths, place, bound_ref, member_ref, inverse_ref),
        "norma": lambda: norm_into(frames, g_attn, normed, 0, 4),
        "normb": lambda: norm_into(frames, g_attn, normed, 4, 8),
        "sendfr": send_frames,
        "normx": lambda: norm_halo(0, 4),
        "normy": lambda: norm_halo(4, 8),
        "laykv": lay_kv,
        "mmkv0": lambda: make_kv(0),
        "mmkv1": lambda: make_kv(1),
        "sendkv": send_kv,
        "layq": lay_q,
        "mmq": make_q,
        "layo": lay_o,
        "att0": lambda: attention(0),
        "att1": lambda: attention(1),
        "att2": lambda: attention(2),
        "att3": lambda: attention(3),
        "mmo": make_after,
        "normc": lambda: norm_into(after, g_conv, normed, 0, 4),
        "normd": lambda: norm_into(after, g_conv, normed, 4, 8),
        "laye": lay_e,
        "mme0": lambda: make_glu(0),
        "mme1": lambda: make_glu(1),
        "mme2": lambda: make_glu(2),
        "sendrim": send_rim,
        "conv0": lambda: conv(1, 3),
        "conv1": lambda: conv(4, 3),
        "lays": lay_s,
        "conv2": conv_edges,
        "mms": make_moved,
        "fin": finish,
    }
    for name in PLAN:
        if name.startswith("start"):
            start(int(name[5:]))
        elif name[0].isdigit():
            groups[int(name[0])].step(int(name[1]))
        else:
            tasks[name]()
    pool(copies, place, part_ref, pool_give, pool_take, sum_ref, sum16, rx, s2, rz, zb, xb, sb, pooled_ref)
    last = pltpu.make_async_copy(pooled_ref, h_pooled, load_sem.at[len(pairs) + 1])
    last.start()
    copies.finish()
    sent["out"].wait()
    last.wait()


def local(frames, lengths, norm_attn, w_query, w_key, w_value, w_out, norm_conv, w_expand, kernel, bn_gain,
          bn_bias, w_shrink, norm_final):
    hbm = pl.BlockSpec(memory_space=pl.ANY)
    block_out, pooled = pl.pallas_call(
        block_kernel,
        out_shape=[
            jax.ShapeDtypeStruct((ROWS, D), BF16),
            jax.ShapeDtypeStruct((NREC, D), BF16),
        ],
        in_specs=[hbm] * 14,
        out_specs=[hbm] * 2,
        scratch_shapes=[
            pltpu.VMEM((ROWS, D), BF16),
            pltpu.VMEM((1, NREC), jnp.int32),
            pltpu.VMEM((D,), F32),
            pltpu.VMEM((24, CH), BF16),
            pltpu.VMEM((24, CH), BF16),
            pltpu.VMEM((24, CH), BF16),
            pltpu.VMEM((12, D), BF16),
            pltpu.VMEM((D,), F32),
            pltpu.VMEM((24, D), BF16),
            pltpu.VMEM((KERNEL, CH), F32),
            pltpu.VMEM((CH,), F32),
            pltpu.VMEM((CH,), F32),
            pltpu.VMEM((12, D), BF16),
            pltpu.VMEM((D,), F32),
            pltpu.VMEM((ROWS, D), BF16),
            pltpu.VMEM((NREC, D), BF16),
            pltpu.VMEM((NZ, NX, 2, 16, COLS), BF16),
            pltpu.VMEM((16, COLS), BF16),
            pltpu.VMEM((D, 2 * CH), BF16),
            pltpu.VMEM((D, CH), BF16),
            pltpu.VMEM((CH, D), BF16),
            pltpu.VMEM((D, 2 * CH), BF16),
            pltpu.VMEM((CH, D), BF16),
            pltpu.VMEM((2, 16, CH), BF16),
            pltpu.VMEM((2, 16, CH), BF16),
            pltpu.VMEM((ROWS, D), BF16),
            pltpu.VMEM((2 * ROWS, D), BF16),
            pltpu.VMEM((ROWS, CH), BF16),
            pltpu.VMEM((3 * ROWS, 2 * CH), BF16),
            pltpu.VMEM((ROWS, CH), BF16),
            pltpu.VMEM((ROWS, D), BF16),
            pltpu.VMEM((ROWS, CH), BF16),
            pltpu.VMEM((CH // 128, ROWS + 32, 128), F32),
            pltpu.VMEM((2, 16, CH), BF16),
            pltpu.VMEM((ROWS, CH), BF16),
            pltpu.VMEM((ROWS, D), F32),
            pltpu.VMEM((2, ROWS, NREC), F32),
            pltpu.VMEM((NREC, ROWS), BF16),
            pltpu.VMEM((NREC, NREC), F32),
            pltpu.VMEM((2, NREC, CH), F32),
            pltpu.VMEM((2, NREC, CH), BF16),
            pltpu.VMEM((NREC, CH), BF16),
            pltpu.VMEM((NREC, CH), F32),
            pltpu.VMEM((NREC, CH), BF16),
            pltpu.VMEM((NX - 1, 32, CH), BF16),
            pltpu.VMEM((NZ, 8, 384), F32),
            pltpu.VMEM((NZ - 1, 8, 384), F32),
            pltpu.VMEM((NZ, 8, 384), F32),
            pltpu.VMEM((NX, 32, CH), BF16),
            pltpu.VMEM((NX, 32, CH), BF16),
            pltpu.SemaphoreType.DMA((N_COPIES,)),
            pltpu.SemaphoreType.DMA((N_COPIES,)),
            pltpu.SemaphoreType.DMA((16,)),
        ],
        compiler_params=pltpu.CompilerParams(
            collective_id=0, has_side_effects=True, vmem_limit_bytes=60 << 20
        ),
        cost_estimate=pl.CostEstimate(flops=5_000_000_000, bytes_accessed=20_000_000, transcendentals=3_000_000),
    )(
        frames, lengths.reshape(1, NREC), norm_attn, w_query, w_key, w_value, w_out,
        norm_conv, w_expand, kernel, bn_gain, bn_bias, w_shrink,
        norm_final,
    )
    return block_out, pooled.astype(F32)


def solution(mesh):
    return jax.shard_map(
        local,
        mesh=mesh,
        in_specs=(
            P(("rep", "seq"), None),
            P("rep"),
            P(),
            P("seq", None),
            P("seq", None),
            P("seq", None),
            P("seq", None),
            P(),
            P("seq", None),
            P(),
            P(),
            P(),
            P("seq", None),
            P(),
        ),
        out_specs=(P(("rep", "seq"), None), P("rep", None)),
        check_vma=False,
    )
```

```python
import jax
import jax.numpy as jnp
from jax import lax
from jax.experimental import pallas as pl
from jax.experimental.pallas import tpu as pltpu
from jax.sharding import PartitionSpec as P

H = 8
HD = 96
KERNEL = 31
HALF = 15
MESH = pl.DeviceIdType.MESH
F32 = jnp.float32
BF16 = jnp.bfloat16
NZ, NX, NY = 8, 4, 4
ROWS = 256
D = 1536
CH = 768
NREC = 128
UNIT = 1152
COLS = 7 * UNIT
GROUPS = (
    (0, 2, (7, 7, 4), ('straight', 'ring', 'ring', 'ring', 'straight')),
    (2, 4, (7, 3, 8), ('straight', 'ring', 'ring', 'ring', 'hops')),
    (4, 6, (5, 5, 8), ('ring', 'ring', 'ring', 'ring', 'straight')),
    (6, 7, (1, 0, 8), ('straight', 'ring', 'hops', 'ring', 'ring')),
)
N_COPIES = 83
PLAN = (
    "start0", "sendfr", "packrest", "bounds", "packos", "01", "start1", "00", "02", "start3", "norma",
    "normb", "01", "11", "12", "start2", "00", "32", "01", "11", "12", "21", "normx", "normy", "10", "22",
    "02", "30", "20", "00", "32", "01", "11", "21", "12", "22", "10", "20", "30", "02", "00", "32", "11",
    "21", "10", "12", "20", "02", "30", "01", "00", "32", "22", "21", "laykv", "12", "10", "mmkv0", "11",
    "20", "mmkv1", "10", "32", "sendkv", "layq", "mmq", "22", "20", "layo", "21", "att0", "att1", "att2",
    "20", "att3", "21", "32", "mmo", "normc", "22", "normd", "laye", "mme0", "mme1", "32", "mme2", "sendrim",
    "conv0", "conv1", "lays", "conv2", "mms", "fin",
)


class Place:
    def __init__(self):
        self.index = lax.axis_index("seq")
        self.z = self.index // 8
        self.x = (self.index // 2) % 4
        self.c = self.index % 2
        self.y = lax.axis_index("rep")

    def at(self, dz=0, dx=0, dc=0, dy=0):
        z = (self.z + dz + NZ) % NZ
        x = (self.x + dx + NX) % NX
        c = (self.c + dc) % 2
        y = (self.y + dy + NY) % NY
        return {"seq": z * 8 + x * 2 + c, "rep": y}

    def beside(self, step):
        return {"seq": (self.index + step + 64) % 64, "rep": self.y}

    def partners(self):
        found = [self.at(dz=k) for k in range(1, NZ)]
        found += [self.at(dx=k) for k in range(1, NX)]
        found += [self.at(dy=k) for k in range(1, NY)]
        found += [self.at(dc=1), self.beside(2 * self.c - 1)]
        return found


class Copies:
    def __init__(self, send_sem, recv_sem):
        self.send_sem, self.recv_sem = send_sem, recv_sem
        self.count = 0
        self.all = []

    def sems(self):
        self.count += 1
        return {"send_sem": self.send_sem.at[self.count - 1], "recv_sem": self.recv_sem.at[self.count - 1]}

    def send(self, src, dst, device):
        copy = pltpu.make_async_remote_copy(
            src_ref=src, dst_ref=dst, device_id=device, device_id_type=MESH, **self.sems()
        )
        copy.start()
        self.all.append(copy)
        return copy

    def finish(self):
        for copy in self.all:
            copy.wait_send()


class Batch:
    def __init__(self, copies, ref, whole, device):
        self.ref, self.sems = ref, copies.sems()
        self.total = self.make(whole, device)
        copies.all.append(self)

    def make(self, region, device):
        part = self.ref.at[region]
        return pltpu.make_async_remote_copy(
            src_ref=part, dst_ref=part, device_id=device, device_id_type=MESH, **self.sems
        )

    def push(self, region, device):
        self.make(region, device).start()

    def wait_recv(self):
        self.total.wait_recv()

    def wait_send(self):
        self.total.wait_send()


class Gather:
    def __init__(self, copies, place, ref, own):
        self.copies, self.place, self.ref, self.own = copies, place, ref, own

    def batch(self, whole):
        return Batch(self.copies, self.ref, whole, self.place.at(dc=1))

    def straight(self, axis, n, region, many, shared):
        place = self.place
        me = {"z": place.z, "x": place.x, "y": place.y}[axis]
        sent = self.batch(many(n - 1))
        for k in range(1, n):
            sent.push(region(me, None), place.at(**{"d" + axis: k}))
        yield
        sent.wait_recv()
        for k in range(1, n):
            shared.push(region((me - k + n) % n, None), place.at(dc=1))

    def hops(self, region, many, shared):
        place = self.place
        me, other = place.z, place.at(dc=1)
        block = lambda k: region((me + k + NZ) % NZ, None)
        sent = self.batch(many(4))
        for k in (1, -1, 2, -2):
            sent.push(block(0), place.at(dz=k))
        yield
        sent.wait_recv()
        sent = self.batch(many(3))
        for k in (1, -1):
            sent.push(block(-2 * k), place.at(dz=k))
        for k in (1, -1):
            half = region((me - 2 * k + NZ) % NZ, 0 if k == 1 else 1)
            if half is not None:
                sent.push(half, place.at(dz=2 * k))
        for k in (1, -1, 2, -2):
            shared.push(block(k), other)
        yield
        sent.wait_recv()
        for k in (3, -3, 4):
            shared.push(block(k), other)

    def ring(self, axis, region, many, shared):
        place = self.place
        n = {"z": NZ, "x": NX, "y": NY}[axis]
        me = {"z": place.z, "x": place.x, "y": place.y}[axis]
        up, down, other = place.at(**{"d" + axis: 1}), place.at(**{"d" + axis: -1}), place.at(dc=1)
        sent = self.batch(many(2))
        sent.push(region(me, None), up)
        sent.push(region(me, None), down)
        for step in range(1, n // 2):
            low, high = (me - step + n) % n, (me + step) % n
            last = step == n // 2 - 1
            yield
            sent.wait_recv()
            sent = self.batch(many(1 if last else 2))
            sent.push(region(low, 0 if last else None), up)
            rest = region(high, 1 if last else None)
            if rest is not None:
                sent.push(rest, down)
            shared.push(region(low, None), other)
            shared.push(region(high, None), other)
        yield
        sent.wait_recv()
        shared.push(region((me + n // 2) % n, None), other)

    def part(self, order, lo, tiles, modes, shared):
        place = self.place
        quarter = tiles // 4 if "y" in order else tiles

        def cut(k, half, count):
            start, size = 0, count * 128
            if half is not None:
                first = (count + 1) // 2 * 128
                start, size = (0, first) if half == 0 else (first, size - first)
            if "y" not in order:
                return pl.ds(lo + start, size)
            return pl.ds(pl.multiple_of(lo + k * (quarter * 128) + start, 128), size)

        done = set()
        for axis in order:

            def region(k, half, axis=axis, done=frozenset(done)):
                at = {"z": place.z, "x": place.x, "y": place.y}
                at[axis] = k
                z = slice(None) if "z" in done else at["z"]
                x = slice(None) if "x" in done else at["x"]
                if half == 1 and quarter == 1:
                    return None
                return (z, x, place.c, slice(None), cut(at["y"], half, quarter))

            def many(count, axis=axis, region=region):
                at = list(region({"z": place.z, "x": place.x, "y": place.y}[axis], None))
                if axis == "y":
                    at[4] = pl.ds(lo, count * quarter * 128)
                else:
                    at["zx".index(axis)] = pl.ds(0, count)
                return tuple(at)

            mode = modes[axis]
            if mode == "hops":
                yield from self.hops(region, many, shared)
            elif mode == "ring":
                yield from self.ring(axis, region, many, shared)
            else:
                yield from self.straight(axis, {"z": NZ, "x": NX, "y": NY}[axis], region, many, shared)
            done.add(axis)

    def start(self, group):
        place = self.place
        first, end, tiles, ways = GROUPS[group]
        lo, hi = first * UNIT, end * UNIT
        quarter = tiles[2] * 32
        mid = hi - 4 * quarter
        shared = self.batch((slice(None), slice(None), place.c, slice(None), pl.ds(lo, hi - lo)))
        spans = []
        if mid > lo:
            spans.append(pl.ds(lo, mid - lo))
        if quarter:
            spans.append(pl.ds(pl.multiple_of(mid + place.y * quarter, 128), quarter))
        for cols in spans:
            region = (place.z, place.x, place.c, slice(None), cols)
            self.ref[region] = self.own[:, cols]
            shared.push(region, place.at(dc=1))
        parts = {}
        for k, (order, count) in enumerate(zip(("xz", "zx", "zxy"), tiles)):
            if count:
                parts[k] = self.part(order, lo, count, {"x": ways[0], "y": ways[1], "z": ways[2 + k]}, shared)
                lo += count * 128
        return Group(parts, shared)


class Group:
    def __init__(self, parts, shared):
        self.parts, self.shared = parts, shared
        for part in parts.values():
            next(part)

    def step(self, k):
        if next(self.parts[k], True) is not None:
            del self.parts[k]

    def finish(self):
        if self.shared is not None:
            self.shared.wait_recv()
        self.shared = None
        return not self.parts


def fold(rows8):
    half = rows8.shape[1] // 2
    return jnp.concatenate([rows8[:, :half], rows8[:, half:]], axis=0)


def pack_own(own_ref, unit, value, first):
    main = jnp.where(first, value[:16], value[8:])
    rest = jnp.where(first, value[16:], value[:8])
    whole = jnp.concatenate([main, fold(rest)], axis=1).astype(BF16)
    own_ref[:, unit * UNIT : (unit + 1) * UNIT] = whole


def unfold(low, high):
    low, high = low.astype(F32), high.astype(F32)
    left = jnp.concatenate([low[:8], high[:8]], axis=0)
    right = jnp.concatenate([low[8:], high[8:]], axis=0)
    return jnp.concatenate([left, right], axis=1).astype(BF16)


def lay_rows(g_ref, unit, w_ref, column):
    lo = unit * UNIT

    @pl.loop(0, NZ)
    def _(z):
        for x in range(NX):
            row = z * 192 + x * 48
            low, high = g_ref[z, x, 0, :, lo : lo + UNIT], g_ref[z, x, 1, :, lo : lo + UNIT]
            for k, value in enumerate((low[:, :CH], unfold(low[:, CH:], high[:, CH:]), high[:, :CH])):
                w_ref[pl.ds(pl.multiple_of(row + 16 * k, 16), 16), column : column + CH] = value


def lay_halves(g_ref, unit, w_ref):
    lo = unit * UNIT

    @pl.loop(0, NZ)
    def _(z):
        for pair in range(2):
            for c in range(2):
                row = z * 96 + pair * 48
                low = g_ref[z, 2 * pair, c, :, lo : lo + UNIT]
                high = g_ref[z, 2 * pair + 1, c, :, lo : lo + UNIT]
                for k, value in enumerate((low[:, :CH], unfold(low[:, CH:], high[:, CH:]), high[:, :CH])):
                    w_ref[pl.ds(pl.multiple_of(row + 16 * k, 16), 16), c * CH : (c + 1) * CH] = value


def norm_rows(values, gain):
    mean = jnp.mean(values, axis=-1, keepdims=True)
    centred = values - mean
    var = jnp.mean(centred * centred, axis=-1, keepdims=True)
    return centred * lax.rsqrt(var + 1e-05) * gain


def norm_into(src, gain, dst, first, end):
    @pl.loop(first, end)
    def _(i):
        rows = pl.ds(pl.multiple_of(i * 32, 32), 32)
        dst[rows, :] = norm_rows(src[rows, :].astype(F32), gain[...].reshape(1, D)).astype(BF16)


def times(x_ref, w_ref, column):
    return jnp.dot(
        x_ref[...], w_ref[:, pl.ds(pl.multiple_of(column, 256), 256)], preferred_element_type=F32
    )


def bounds(len_ref, place, bound_ref, member_ref, inverse_ref):
    lengths = len_ref[...].astype(F32)
    row = lax.broadcasted_iota(jnp.int32, (NREC, NREC), 0)
    col = lax.broadcasted_iota(jnp.int32, (NREC, NREC), 1)
    before = (row <= col).astype(BF16)
    wide = jnp.broadcast_to(lengths, (NREC, NREC))
    ends = jnp.dot(wide.astype(BF16), before, preferred_element_type=F32)
    first = (place.index * ROWS).astype(F32)
    t = lax.broadcasted_iota(jnp.int32, (ROWS, NREC), 0).astype(F32) + first
    end_row = jnp.broadcast_to(ends[:1], (ROWS, NREC))
    begin = jnp.max(jnp.where(end_row <= t, end_row, 0.0), axis=1, keepdims=True)
    finish = jnp.min(jnp.where(end_row > t, end_row, 65536.0), axis=1, keepdims=True)
    bound_ref[0] = jnp.broadcast_to(begin, (ROWS, NREC)) - t
    bound_ref[1] = jnp.broadcast_to(finish, (ROWS, NREC)) - t
    eye = row == col
    end_col = jnp.sum(jnp.where(eye, ends, 0.0), axis=1, keepdims=True)
    len_col = jnp.sum(jnp.where(eye, wide, 0.0), axis=1, keepdims=True)
    inverse_ref[...] = jnp.broadcast_to(1.0 / len_col, (NREC, NREC))
    at = lax.broadcasted_iota(jnp.int32, (NREC, ROWS), 1).astype(F32) + first
    inside = (at < end_col) & (at >= end_col - len_col)
    member_ref[...] = inside.astype(F32).astype(BF16)


def attend(i, q_ref, kv_ref, bound_ref, ctx_ref):
    factor = 1.4426950408889634 / HD**0.5
    span = 640

    top, lane0 = (i // 2) * 128, (i % 2) * 384
    rows = pl.ds(pl.multiple_of(top, 128), 128)
    window = pl.ds(pl.multiple_of(top, 128), span)
    offset = lax.broadcasted_iota(jnp.int32, (128, span), 1) - lax.broadcasted_iota(jnp.int32, (128, span), 0)
    offset = (offset - ROWS).astype(F32)
    inside = (offset >= bound_ref[0, rows, :1]) & (offset < bound_ref[1, rows, :1])
    bias = jnp.where(inside, 0.0, -1e30)
    outs = []
    for h in range(4):
        lo, hi = h * HD, (h + 1) * HD
        a, b = lo // 128 * 128, (hi + 127) // 128 * 128
        lane = lax.broadcasted_iota(jnp.int32, (128, b - a), 1) + a
        cols = pl.ds(pl.multiple_of(lane0 + a, 128), b - a)
        q = q_ref[rows, cols]
        q = jnp.where((lane >= lo) & (lane < hi), q.astype(F32), 0.0).astype(BF16)
        score = lax.dot_general(
            q, kv_ref[window, cols], (((1,), (1,)), ((), ())), preferred_element_type=F32
        )
        score = score + bias
        peak = jnp.max(score, axis=1, keepdims=True)
        expo = jnp.exp2((score - peak) * factor)
        total = jnp.sum(expo, axis=1, keepdims=True)
        values = kv_ref[window, pl.ds(pl.multiple_of(CH + lane0 + a, 128), b - a)]
        out = jnp.dot(expo.astype(BF16), values, preferred_element_type=F32)
        outs.append((a, out / total))
    for tile in range(3):
        lane = lax.broadcasted_iota(jnp.int32, (128, 128), 1)
        at = tile * 128
        one, two = outs[tile], outs[tile + 1]
        left = one[1][:, at - one[0] : at - one[0] + 128]
        right = two[1][:, at - two[0] : at - two[0] + 128]
        whole = jnp.where(lane < (tile + 1) * HD - at, left, right).astype(BF16)
        ctx_ref[rows, pl.ds(pl.multiple_of(lane0 + at, 128), 128)] = whole


def convolve(first, count, glu_ref, bound_ref, taps, gain, bias, act_ref):
    @pl.loop(0, count)
    def _(i):
        top = pl.multiple_of((i + first) * 32, 32)
        rows = pl.ds(top, 32)
        behind, ahead = bound_ref[0, rows, :], bound_ref[1, rows, :]
        for tile in range(CH // 128):
            lanes = slice(tile * 128, (tile + 1) * 128)
            depth = jnp.zeros((32, 128), F32)
            for j in range(KERNEL):
                source = glu_ref[tile, pl.ds(top + j + 1, 32), :]
                if j < HALF:
                    source = jnp.where(behind <= float(j - HALF), source, 0.0)
                elif j > HALF:
                    source = jnp.where(ahead > float(j - HALF), source, 0.0)
                depth = depth + taps[j : j + 1, lanes] * source
            moved = depth * gain[lanes].reshape(1, 128) + bias[lanes].reshape(1, 128)
            act_ref[rows, lanes] = (moved * jax.nn.sigmoid(moved)).astype(BF16)


def pool(copies, place, part_ref, give, take, sum_ref, sum16, rx, s2, rz, zb, xb, sb, out_ref):
    c = place.c

    def exchange(axis, n, src, dst, size):
        sems = copies.sems()

        def make(src, dst, device):
            return pltpu.make_async_remote_copy(
                src_ref=src, dst_ref=dst, device_id=device, device_id_type=MESH, **sems
            )

        for k in range(1, n):
            make(src(k), dst(k), place.at(**{"d" + axis: k})).start()
        total = make(size, size, place.at(dc=1))
        copies.all.append(total)
        return total

    def third(n):
        cols = slice(n * 256, (n + 1) * 256)
        span = pl.ds(n * 256, 256)
        copy = copies.send(give.at[1 - c, :, span], take.at[:, span], place.at(dc=1))
        yield
        copy.wait_recv()
        sum_ref[:, cols] = part_ref[c, :, cols] + take[:, cols].astype(F32)
        sum16[:, cols] = sum_ref[:, cols].astype(BF16)

        def theirs(k):
            return sum16.at[pl.ds(pl.multiple_of((place.x + k) % NX * 32, 32), 32), span]

        copy = exchange("x", NX, theirs, lambda k: rx.at[n, k - 1], rx.at[n])
        yield
        copy.wait_recv()
        total = sum_ref[pl.ds(pl.multiple_of(place.x * 32, 32), 32), cols]
        for k in range(NX - 1):
            total = total + rx[n, k].astype(F32)
        for j in range(NZ):
            s2[n, j] = total[8 * (j // 2) : 8 * (j // 2) + 8, 128 * (j % 2) : 128 * (j % 2) + 128]
        copy = exchange("z", NZ, lambda k: s2.at[n, (place.z + k) % NZ], lambda k: rz.at[n, k - 1], rz.at[n])
        yield
        copy.wait_recv()
        total = s2[n, place.z]
        for k in range(NZ - 1):
            total = total + rz[n, k]
        zb[n, place.z] = total
        copy = exchange("z", NZ, lambda k: zb.at[n, place.z], lambda k: zb.at[n, place.z], rz.at[n])
        yield
        copy.wait_recv()
        parts = [jnp.concatenate([zb[n, 2 * j], zb[n, 2 * j + 1]], axis=1) for j in range(4)]
        xb[n, place.x] = jnp.concatenate(parts, axis=0).astype(BF16)
        copy = exchange("x", NX, lambda k: xb.at[n, place.x], lambda k: xb.at[n, place.x], rx.at[n])
        yield
        copy.wait_recv()
        copy = copies.send(xb.at[n], sb.at[n], place.at(dc=1))
        yield
        copy.wait_recv()
        for k in range(NX):
            rows = slice(32 * k, 32 * k + 32)
            out_ref[rows, pl.ds(pl.multiple_of(c * CH + n * 256, 256), 256)] = xb[n, k]
            out_ref[rows, pl.ds(pl.multiple_of((1 - c) * CH + n * 256, 256), 256)] = sb[n, k]

    live = [third(n) for n in range(3)]
    while live:
        live = [one for one in live if next(one, True) is None]


def block_kernel(
    h_frames, h_lengths, h_g_attn, h_wq, h_wk, h_wv, h_wo, h_g_conv, h_we, h_taps, h_bn_gain, h_bn_bias, h_ws, h_g_final,
    h_out, h_pooled,
    frames, lengths, g_attn, wq, wk, wv, wo, g_conv, we, taps, bn_gain, bn_bias, ws, g_final, out_ref, pooled_ref,
    g_ref, own_ref, w_kv, w_q, w_o, w_e, w_s, give, take, halo, normed, query, kv, ctx, after, glu16, glu_ref, rim, act,
    moved, bound_ref, member_ref, inverse_ref, part_ref, pool_give, pool_take, sum_ref, sum16, rx, s2, rz, zb, xb, sb,
    send_sem, recv_sem, load_sem,
):
    place = Place()
    barrier = pltpu.get_barrier_semaphore()
    partners = place.partners()
    for partner in partners:
        pl.semaphore_signal(barrier, inc=1, device_id=partner, device_id_type=MESH)
    pairs = (
        (h_wk, wk), (h_wv, wv), (h_wo, wo), (h_ws, ws), (h_frames, frames), (h_wq, wq), (h_we, we), (h_g_attn, g_attn),
        (h_lengths, lengths), (h_g_conv, g_conv), (h_taps, taps), (h_bn_gain, bn_gain), (h_bn_bias, bn_bias),
        (h_g_final, g_final),
    )
    loads = [pltpu.make_async_copy(src, dst, load_sem.at[k]) for k, (src, dst) in enumerate(pairs)]
    for load in loads:
        load.start()
    lead = place.c == 0
    for load in loads[:4]:
        load.wait()
    pack_own(own_ref, 0, wk[...].astype(F32), lead)
    pack_own(own_ref, 1, wv[...].astype(F32), lead)
    for k, ref in enumerate((wo, ws)):
        value = ref[...].astype(F32)
        theirs = jnp.where(lead, value[:, CH:], value[:, :CH])
        give[k] = jnp.concatenate([theirs, jnp.zeros((4, CH), F32)], axis=0).astype(BF16)
    for load in loads[4:]:
        load.wait()
    pl.semaphore_wait(barrier, len(partners))

    copies = Copies(send_sem, recv_sem)
    gather = Gather(copies, place, g_ref, own_ref)
    groups, sent = {}, {}

    def start(g):
        groups[g] = gather.start(g)
        if g == 0:
            sent["side"] = copies.send(give, take, place.at(dc=1))

    def pack_rest():
        pack_own(own_ref, 2, wq[...].astype(F32), lead)
        pack_own(own_ref, 4, we[:, :CH].astype(F32), lead)
        pack_own(own_ref, 5, we[:, CH:].astype(F32), lead)

    def pack_halves():
        sent["side"].wait_recv()
        for k, (unit, ref) in enumerate(((3, wo), (6, ws))):
            value = ref[...].astype(F32)
            own = jnp.where(lead, value[:, :CH], value[:, CH:])
            got = take[k].astype(F32)[:12]
            both = jnp.where(lead, jnp.concatenate([own, got], axis=0), jnp.concatenate([got, own], axis=0))
            pack_own(own_ref, unit, both, place.x % 2 == 0)

    def arrived(unit):
        for g, (first, end, _, _) in enumerate(GROUPS):
            if first <= unit < end:
                assert groups[g].finish()

    def lay_kv():
        arrived(0)
        lay_rows(g_ref, 0, w_kv, 0)
        lay_rows(g_ref, 1, w_kv, CH)

    far = pl.ds(pl.multiple_of(place.c * (2 * ROWS), ROWS), ROWS)

    def send_frames():
        sent["frames"] = copies.send(frames, halo, place.beside(2 * place.c - 1))

    def norm_halo(first, end):
        if first == 0:
            sent["frames"].wait_recv()
        norm_into(halo, g_attn, normed.at[pl.ds(ROWS, ROWS)], first, end)

    def make_kv(half):
        @pl.loop(half * 3, half * 3 + 3)
        def _(n):
            cols = pl.ds(pl.multiple_of(n * 256, 256), 256)
            both = times(normed, w_kv, n * 256).astype(BF16)
            kv[ROWS : 2 * ROWS, cols] = both[:ROWS]
            kv[far, cols] = both[ROWS:]

    def send_kv():
        sent["kv"] = copies.send(kv.at[pl.ds(ROWS, ROWS)], kv.at[far], place.at(dc=1))

    def lay_q():
        arrived(2)
        lay_rows(g_ref, 2, w_q, 0)

    def make_q():
        @pl.loop(0, 3)
        def _(n):
            query[:, pl.ds(pl.multiple_of(n * 256, 256), 256)] = times(normed.at[pl.ds(0, ROWS)], w_q, n * 256).astype(BF16)

    def lay_o():
        arrived(3)
        lay_halves(g_ref, 3, w_o)

    def attention(k):
        if k == 0:
            sent["kv"].wait_recv()
        attend(k, query, kv, bound_ref, ctx)

    def make_after():
        @pl.loop(0, 6)
        def _(n):
            cols = pl.ds(pl.multiple_of(n * 256, 256), 256)
            after[:, cols] = (frames[:, cols].astype(F32) + times(ctx, w_o, n * 256)).astype(BF16)

    def lay_e():
        arrived(4)
        lay_rows(g_ref, 4, w_e, 0)
        lay_rows(g_ref, 5, w_e, CH)

    def make_glu(n):
        gate = times(normed.at[pl.ds(0, ROWS)], w_e, CH + n * 256)
        value = times(normed.at[pl.ds(0, ROWS)], w_e, n * 256)
        glu = (value * jax.nn.sigmoid(gate)).astype(BF16)
        glu16[:, n * 256 : n * 256 + 256] = glu
        wide = glu.astype(F32)
        glu_ref[2 * n, 16 : 16 + ROWS, :] = wide[:, :128]
        glu_ref[2 * n + 1, 16 : 16 + ROWS, :] = wide[:, 128:]

    def send_rim():
        sent["rim0"] = copies.send(glu16.at[pl.ds(0, 16)], rim.at[1], place.beside(-1))
        sent["rim1"] = copies.send(glu16.at[pl.ds(ROWS - 16, 16)], rim.at[0], place.beside(1))

    def conv(first, count):
        convolve(first, count, glu_ref, bound_ref, taps, bn_gain, bn_bias, act)

    def conv_edges():
        sent["rim0"].wait_recv()
        sent["rim1"].wait_recv()
        for tile in range(CH // 128):
            lanes = slice(tile * 128, (tile + 1) * 128)
            glu_ref[tile, :16, :] = rim[0, :, lanes].astype(F32)
            glu_ref[tile, 16 + ROWS :, :] = rim[1, :, lanes].astype(F32)
        conv(0, 1)
        conv(7, 1)

    def lay_s():
        arrived(6)
        lay_halves(g_ref, 6, w_s)

    def make_moved():
        @pl.loop(0, 6)
        def _(n):
            cols = pl.ds(pl.multiple_of(n * 256, 256), 256)
            moved[:, cols] = after[:, cols].astype(F32) + times(act, w_s, n * 256)

    def finish():
        norm_into(moved, g_final, out_ref, 0, 8)
        sent["out"] = pltpu.make_async_copy(out_ref, h_out, load_sem.at[len(pairs)])
        sent["out"].start()
        for h in range(2):
            for n in range(3):
                cols = slice(h * CH + n * 256, h * CH + n * 256 + 256)
                sums = jnp.dot(member_ref[...], out_ref[:, cols], preferred_element_type=F32) * inverse_ref[:, :1]
                part_ref[h, :, n * 256 : n * 256 + 256] = sums
                pool_give[h, :, n * 256 : n * 256 + 256] = sums.astype(BF16)

    tasks = {
        "packrest": pack_rest,
        "packos": pack_halves,
        "bounds": lambda: bounds(lengths, place, bound_ref, member_ref, inverse_ref),
        "norma": lambda: norm_into(frames, g_attn, normed, 0, 4),
        "normb": lambda: norm_into(frames, g_attn, normed, 4, 8),
        "sendfr": send_frames,
        "normx": lambda: norm_halo(0, 4),
        "normy": lambda: norm_halo(4, 8),
        "laykv": lay_kv,
        "mmkv0": lambda: make_kv(0),
        "mmkv1": lambda: make_kv(1),
        "sendkv": send_kv,
        "layq": lay_q,
        "mmq": make_q,
        "layo": lay_o,
        "att0": lambda: attention(0),
        "att1": lambda: attention(1),
        "att2": lambda: attention(2),
        "att3": lambda: attention(3),
        "mmo": make_after,
        "normc": lambda: norm_into(after, g_conv, normed, 0, 4),
        "normd": lambda: norm_into(after, g_conv, normed, 4, 8),
        "laye": lay_e,
        "mme0": lambda: make_glu(0),
        "mme1": lambda: make_glu(1),
        "mme2": lambda: make_glu(2),
        "sendrim": send_rim,
        "conv0": lambda: conv(1, 3),
        "conv1": lambda: conv(4, 3),
        "lays": lay_s,
        "conv2": conv_edges,
        "mms": make_moved,
        "fin": finish,
    }
    for name in PLAN:
        if name.startswith("start"):
            start(int(name[5:]))
        elif name[0].isdigit():
            groups[int(name[0])].step(int(name[1]))
        else:
            tasks[name]()
    pool(copies, place, part_ref, pool_give, pool_take, sum_ref, sum16, rx, s2, rz, zb, xb, sb, pooled_ref)
    last = pltpu.make_async_copy(pooled_ref, h_pooled, load_sem.at[len(pairs) + 1])
    last.start()
    copies.finish()
    sent["out"].wait()
    last.wait()


def local(frames, lengths, norm_attn, w_query, w_key, w_value, w_out, norm_conv, w_expand, kernel, bn_gain,
          bn_bias, w_shrink, norm_final):
    hbm = pl.BlockSpec(memory_space=pl.ANY)
    block_out, pooled = pl.pallas_call(
        block_kernel,
        out_shape=[
            jax.ShapeDtypeStruct((ROWS, D), BF16),
            jax.ShapeDtypeStruct((NREC, D), BF16),
        ],
        in_specs=[hbm] * 14,
        out_specs=[hbm] * 2,
        scratch_shapes=[
            pltpu.VMEM((ROWS, D), BF16),
            pltpu.VMEM((1, NREC), jnp.int32),
            pltpu.VMEM((D,), F32),
            pltpu.VMEM((24, CH), BF16),
            pltpu.VMEM((24, CH), BF16),
            pltpu.VMEM((24, CH), BF16),
            pltpu.VMEM((12, D), BF16),
            pltpu.VMEM((D,), F32),
            pltpu.VMEM((24, D), BF16),
            pltpu.VMEM((KERNEL, CH), F32),
            pltpu.VMEM((CH,), F32),
            pltpu.VMEM((CH,), F32),
            pltpu.VMEM((12, D), BF16),
            pltpu.VMEM((D,), F32),
            pltpu.VMEM((ROWS, D), BF16),
            pltpu.VMEM((NREC, D), BF16),
            pltpu.VMEM((NZ, NX, 2, 16, COLS), BF16),
            pltpu.VMEM((16, COLS), BF16),
            pltpu.VMEM((D, 2 * CH), BF16),
            pltpu.VMEM((D, CH), BF16),
            pltpu.VMEM((CH, D), BF16),
            pltpu.VMEM((D, 2 * CH), BF16),
            pltpu.VMEM((CH, D), BF16),
            pltpu.VMEM((2, 16, CH), BF16),
            pltpu.VMEM((2, 16, CH), BF16),
            pltpu.VMEM((ROWS, D), BF16),
            pltpu.VMEM((2 * ROWS, D), BF16),
            pltpu.VMEM((ROWS, CH), BF16),
            pltpu.VMEM((3 * ROWS, 2 * CH), BF16),
            pltpu.VMEM((ROWS, CH), BF16),
            pltpu.VMEM((ROWS, D), BF16),
            pltpu.VMEM((ROWS, CH), BF16),
            pltpu.VMEM((CH // 128, ROWS + 32, 128), F32),
            pltpu.VMEM((2, 16, CH), BF16),
            pltpu.VMEM((ROWS, CH), BF16),
            pltpu.VMEM((ROWS, D), F32),
            pltpu.VMEM((2, ROWS, NREC), F32),
            pltpu.VMEM((NREC, ROWS), BF16),
            pltpu.VMEM((NREC, NREC), F32),
            pltpu.VMEM((2, NREC, CH), F32),
            pltpu.VMEM((2, NREC, CH), BF16),
            pltpu.VMEM((NREC, CH), BF16),
            pltpu.VMEM((NREC, CH), F32),
            pltpu.VMEM((NREC, CH), BF16),
            pltpu.VMEM((3, NX - 1, 32, 256), BF16),
            pltpu.VMEM((3, NZ, 8, 128), F32),
            pltpu.VMEM((3, NZ - 1, 8, 128), F32),
            pltpu.VMEM((3, NZ, 8, 128), F32),
            pltpu.VMEM((3, NX, 32, 256), BF16),
            pltpu.VMEM((3, NX, 32, 256), BF16),
            pltpu.SemaphoreType.DMA((N_COPIES,)),
            pltpu.SemaphoreType.DMA((N_COPIES,)),
            pltpu.SemaphoreType.DMA((16,)),
        ],
        compiler_params=pltpu.CompilerParams(
            collective_id=0, has_side_effects=True, vmem_limit_bytes=60 << 20
        ),
        cost_estimate=pl.CostEstimate(flops=5_000_000_000, bytes_accessed=20_000_000, transcendentals=3_000_000),
    )(
        frames, lengths.reshape(1, NREC), norm_attn, w_query, w_key, w_value, w_out,
        norm_conv, w_expand, kernel, bn_gain, bn_bias, w_shrink,
        norm_final,
    )
    return block_out, pooled.astype(F32)


def solution(mesh):
    return jax.shard_map(
        local,
        mesh=mesh,
        in_specs=(
            P(("rep", "seq"), None),
            P("rep"),
            P(),
            P("seq", None),
            P("seq", None),
            P("seq", None),
            P("seq", None),
            P(),
            P("seq", None),
            P(),
            P(),
            P(),
            P("seq", None),
            P(),
        ),
        out_specs=(P(("rep", "seq"), None), P("rep", None)),
        check_vma=False,
    )
```
